32 devices in a mesh: parts: 2 (over x), gz: 8 (over z, y), view: 2 (over core).
Axes of the slice: x: 2, y: 2, z: 4, core: 2. Of those that a mesh axis runs over, the one named last changes fastest.
Arguments:
- observed: bfloat16 [8, 64, 256, 256], P('view', 'parts', 'gz'), parts along dimension 1, may hold values from 0.19921875 to 2
- initial: float32 [64, 256, 256], P('parts', 'gz'), parts along dimension 0, may hold values from 0.5 to 2
- psf_taps: float32 [8, 3, 15], replicated, may hold values from 0.05 to 1
- view_shifts: int32 [8, 2], replicated, may hold values from -7 to 7
- view_map: int32 [8], replicated, may hold values from 0 to 7, each once
Outputs:
- estimate: float32 [64, 256, 256], P('parts', 'gz'), parts along dimension 0
- surfaces: float32 [8, 64, 256, 256], P('view', 'parts', 'gz'), parts along dimension 1
The draws below stay inside these ranges and needn't reach their ends.
There are 2 independent parts, one for each index of `parts`. The reference program is written for one: setup_inputs(seed, part) draws one part's arguments, and reference() takes and returns one part's arrays. A program takes and returns all parts, laid end to end along the dimension named above; an argument that names none is the same for every part. Nothing has to cross between parts.
Inputs may be any that keep to these rules, and one draw needn't show every extreme that they name: `view_map`: each view number stands in exactly one slot; view 0 is the reference view.
All inputs are finite; a program needn't handle non-finite values.
Results may differ from the reference program's by a relative error of at most 0.0014.
Values may be sent and summed in bfloat16 or wider, within the bound.
A program may use at most 128 MiB of HBM per device.

```python
import math
import jax
import jax.numpy as jnp
from jax import lax

VIEWS = 8
ZS = 32
BY = 256
BX = 256
ITERS = 2
X = 256


def with_ends(values, key, low, high):
    shape = values.shape
    spot = [jax.random.randint(jax.random.fold_in(key, axis), (), 0, shape[axis]) for axis in range(len(shape))]
    values = values.at[tuple(spot)].set(low)
    longest = shape.index(max(shape))
    spot[longest] = (spot[longest] + 1) % shape[longest]
    return values.at[tuple(spot)].set(high)


def block_levels(own_key, shape, cuts, least, high):
    gain = 1.0
    for axis_at, parts in cuts:
        steps = jax.random.uniform(jax.random.fold_in(jax.random.fold_in(own_key, 6), axis_at), (parts,), jnp.float32, least / len(cuts), high / len(cuts))
        gain = gain * jnp.repeat(jnp.exp(steps), shape[axis_at] // parts).reshape((-1,) + (1,) * (len(shape) - 1 - axis_at))
    return gain


def setup_inputs(seed: int = 0, part: int = 0) -> dict:
    key_list = jax.random.split(jax.random.key(seed), 6)
    part_splits = jax.random.split(jax.random.fold_in(key_list[5], part), 6)
    return {
        "observed": jnp.clip(0.19921875 + 1.8007812 * jax.random.uniform(part_splits[0], (VIEWS, ZS, BY, X), jnp.float32) ** block_levels(part_splits[0], (VIEWS, ZS, BY, X), ((0, 2), (2, 8)), -0.2, 0.2), 0.19921875, 2.0).astype(jnp.bfloat16),
        "initial": jnp.clip(jnp.exp(math.log(2.0) - 1.3862944 * jax.random.uniform(part_splits[1], (ZS, BY, X), jnp.float32) ** block_levels(part_splits[1], (ZS, BY, X), ((1, 8),), -0.2, 0.2)), 0.5, 2.0),
        "psf_taps": jnp.clip(jnp.exp(jax.random.uniform(key_list[2], (VIEWS, 3, 15), jnp.float32, math.log(0.05), math.log(1.0))), 0.05, 1.0),
        "view_shifts": with_ends(jax.random.randint(key_list[3], (VIEWS, 2), -7, 8), jax.random.fold_in(key_list[3], 1), -7, 7).astype(jnp.int32),
        "view_map": jax.random.permutation(key_list[4], VIEWS).astype(jnp.int32),
    }


def blur_axis(volume, filter_taps, offset_cells, along_axis, orient):
    extent = volume.shape[along_axis]
    widths = [(15, 15) if dim_index == along_axis else (0, 0) for dim_index in range(volume.ndim)]
    padded = jnp.pad(volume, widths)
    summed = jnp.zeros(volume.shape, jnp.float32)
    for tap_index in range(15):
        begin = (15 + orient * (tap_index - 7 + offset_cells)).astype(jnp.int32)
        summed = summed + filter_taps[tap_index] * lax.dynamic_slice_in_dim(padded, begin, extent, along_axis)
    return summed


def blur_view(volume, filter_rows, shift_pair, orient):
    zero_shift = jnp.zeros((), jnp.int32)
    section_rows = blur_axis(volume, filter_rows[1], zero_shift, 1, orient)
    section_depth = blur_axis(section_rows, filter_rows[0], shift_pair[0].astype(jnp.int32), 0, orient)
    return blur_axis(section_depth, filter_rows[2], shift_pair[1].astype(jnp.int32), 2, orient)


def reference(observed, initial, psf_taps, view_shifts, view_map):
    volumes = observed.astype(jnp.float32)
    view_count, depth_cells, row_count, width_cells = volumes.shape
    blocked = volumes.reshape(view_count, depth_cells, row_count, width_cells // BX, BX)
    spectra = jnp.fft.fftn(blocked, axes=(1, 2, 4), norm="ortho")
    ref_slot = jnp.sum(jnp.where(view_map == 0, jnp.arange(VIEWS, dtype=jnp.int32), 0)).astype(jnp.int32)
    ref_spec = spectra[ref_slot]
    cross = spectra * jnp.conj(ref_spec) / (jnp.abs(spectra) * jnp.abs(ref_spec) + 1.0)
    surfaces = jnp.real(jnp.fft.ifftn(cross, axes=(1, 2, 4), norm="ortho"))
    surfaces = surfaces.reshape(volumes.shape).astype(jnp.float32)
    estimate = initial
    for iteration in range(ITERS):
        product = jnp.ones(estimate.shape, jnp.float32)
        for slot_index in range(VIEWS):
            view_id = view_map[slot_index]
            filter_rows = psf_taps[view_id]
            shift_pair = view_shifts[view_id]
            blurred = blur_view(estimate, filter_rows, shift_pair, 1)
            ratio_field = volumes[slot_index] / blurred
            product = product * blur_view(ratio_field, filter_rows, shift_pair, -1)
        estimate = estimate * jnp.exp(jnp.log(product) / VIEWS)
    return estimate, surfaces
```

```python
import functools
import math

import jax
import jax.numpy as jnp
import ml_dtypes
import numpy as np
from jax import lax
from jax.experimental import pallas as pl
from jax.experimental.pallas import tpu as pltpu
from jax.sharding import PartitionSpec as P

VIEWS = 8
BX = 256
ITERS = 2
TAPS = 15
SUB = 8
CENTRE = 1.1
F32 = jnp.float32
BF16 = jnp.bfloat16
SENT = jnp.float16
LIMIT = 56 * 1024 * 1024


def two(table):
    high = table.astype(ml_dtypes.bfloat16)
    low = (table - high.astype(np.float64)).astype(ml_dtypes.bfloat16)
    return np.stack([high, low])


def depth_order(depth):
    order = [0, depth // 2]
    for k in range(1, depth // 2):
        order += [k, depth - k]
    return np.array(order)


def phase_tables(rows, columns, length):
    angles = 2.0 * math.pi / length * (np.outer(rows, columns) % length)
    return np.cos(angles), np.sin(angles)


@functools.lru_cache(None)
def tables(depth, by, bx):
    half = bx // 2
    norm = 1.0 / math.sqrt(depth * by * bx)
    c, s = phase_tables(np.arange(bx), np.arange(half), bx)
    alternate = 1.0 - 2.0 * (np.arange(bx) % 2)
    imag = -s
    imag[:, 0] = alternate
    x_forward = np.concatenate([c, imag], 1)
    weights = np.where(np.arange(half) == 0, 1.0, 2.0)
    imag = -s * weights
    imag[:, 0] = alternate
    x_back = np.concatenate([c * weights, imag], 1).T * norm
    zc, zs = phase_tables(depth_order(depth), np.arange(depth), depth)
    eye = np.eye(SUB)
    yc, ys = phase_tables(np.arange(by), np.arange(by), by)
    return dict(
        x_forward=two(x_forward),
        x_back=two(x_back),
        z_forward=np.stack([two(np.kron(zc, eye)), two(np.kron(zs, eye))]),
        z_back=np.stack([two(np.kron(zc.T, eye)), two(np.kron(zs.T, eye))]),
        y_forward=np.stack([two(yc * norm), two(ys * norm)]),
        y_back=np.stack([two(yc), two(ys)]),
    )


def dot(a, b):
    return jnp.dot(a, b, preferred_element_type=F32)


def split(a):
    high = a.astype(BF16)
    return high, (a - high.astype(F32)).astype(BF16)


def left_mix(table, field):
    high, low = field
    return dot(table[0], high) + dot(table[0], low) + dot(table[1], high)


def right_mix(field, table):
    high, low = field
    return dot(high, table[0]) + dot(low, table[0]) + dot(high, table[1])


def params():
    return pltpu.CompilerParams(vmem_limit_bytes=LIMIT)


def cost(flops, bytes_accessed, transcendentals=0):
    return pl.CostEstimate(
        flops=int(flops), bytes_accessed=int(bytes_accessed), transcendentals=int(transcendentals)
    )


def whole(array):
    zeros = (0,) * array.ndim
    return pl.BlockSpec(array.shape, lambda *_: zeros)


def forward_kernel(obs_ref, x_ref, z_ref, out_ref, held):
    _, depth, rows, width = obs_ref.shape
    half = width // 2
    group, _, _, part, _, _ = out_ref.shape
    lane = lax.broadcasted_iota(jnp.int32, (1, width), 1)
    centre = jnp.where(lane == 0, CENTRE * width, 0.0).astype(F32)
    flat = obs_ref[0].reshape(depth * rows, width)
    mixed = dot(flat, x_ref[0]) + dot(flat, x_ref[1]) - centre
    mixed = mixed.reshape(depth, rows, width)
    for at in range(0, rows, SUB):
        field = split(mixed[:, at : at + SUB, :].reshape(depth * SUB, width))
        cos_part = left_mix(z_ref[0], field)
        sin_part = left_mix(z_ref[1], field)
        real = cos_part[:, :half] + sin_part[:, half:]
        imag = cos_part[:, half:] - sin_part[:, :half]
        held[0, :, at : at + SUB, :] = real.reshape(depth, SUB, half)
        held[1, :, at : at + SUB, :] = imag.reshape(depth, SUB, half)
    for c in range(2):
        out_ref[:, 0, c] = held[c].reshape(group, part, rows, half).astype(out_ref.dtype)


def forward_spectra(observed, group, t):
    views, depth, rows, width = observed.shape
    part = depth // group
    shape = (group, views, 2, part, rows, width // 2)
    x_table, z_table = jnp.asarray(t["x_forward"]), jnp.asarray(t["z_forward"])
    return pl.pallas_call(
        forward_kernel,
        grid=(views,),
        out_shape=jax.ShapeDtypeStruct(shape, F32),
        in_specs=[
            pl.BlockSpec((1,) + observed.shape[1:], lambda v: (v, 0, 0, 0)),
            whole(x_table),
            whole(z_table),
        ],
        out_specs=pl.BlockSpec((group, 1) + shape[2:], lambda v: (0, v, 0, 0, 0, 0)),
        scratch_shapes=[pltpu.VMEM((2, depth, rows, width // 2), F32)],
        compiler_params=params(),
        cost_estimate=cost(observed.size * 256 * 2 * 8, observed.size * 4),
        name="spectra_x_z",
    )(observed, x_table, z_table)


def cross_kernel(depth, first_ref, spec_ref, ref_ref, fwd_ref, back_ref, out_ref, held):
    group, _, _, _, rows, half = spec_ref.shape
    by = group * rows
    pair = pl.program_id(0)
    alone = jnp.logical_and(first_ref[0] == 1, pair == 0)
    lane0 = lax.broadcasted_iota(jnp.int32, (by, half), 1) == 0
    row0 = lax.broadcasted_iota(jnp.int32, (by, half), 0) == 0
    total = CENTRE * math.sqrt(depth * by * 2 * half)
    origin = jnp.logical_and(lane0, row0)

    def spectrum(ref):
        straight, turned = [], []
        for k in range(2):
            real = ref[:, 0, 0, k].astype(F32).reshape(by, half)
            imag = ref[:, 0, 1, k].astype(F32).reshape(by, half)
            field = split(jnp.concatenate([real, imag], 1))
            cos_part = left_mix(fwd_ref[0], field)
            sin_part = left_mix(fwd_ref[1], field)
            cos_real = cos_part[:, :half]
            if k == 0:
                cos_real = cos_real + jnp.where(jnp.logical_and(origin, alone), total, 0.0)
            straight.append((cos_real + sin_part[:, half:], cos_part[:, half:] - sin_part[:, :half]))
            turned.append((cos_real - sin_part[:, half:], cos_part[:, half:] + sin_part[:, :half]))
        out = []
        for k in range(2):
            real, imag = straight[k]
            other_real = jnp.where(alone, turned[k][0], turned[1 - k][0])
            other_imag = jnp.where(alone, turned[k][1], turned[1 - k][1])
            out.append(
                (
                    jnp.where(lane0, 0.5 * (real + other_real), real),
                    jnp.where(lane0, 0.5 * (imag - other_imag), imag),
                    0.5 * (imag + other_imag),
                    0.5 * (other_real - real),
                )
            )
        return out

    @pl.when(pl.program_id(1) == 0)
    def _():
        for k, member in enumerate(spectrum(ref_ref)):
            for i in range(4):
                held[k, i] = member[i]

    def cross(sr, si, rr, ri):
        magnitude = jnp.sqrt((sr * sr + si * si) * (rr * rr + ri * ri))
        scale = 1.0 / (magnitude + 1.0)
        return (sr * rr + si * ri) * scale, (si * rr - sr * ri) * scale

    for k, member in enumerate(spectrum(spec_ref)):
        real, imag = cross(member[0], member[1], held[k, 0], held[k, 1])
        top_real, top_imag = cross(member[2], member[3], held[k, 2], held[k, 3])
        real = jnp.where(lane0, real - top_imag, real)
        imag = jnp.where(lane0, imag + top_real, imag)
        field = split(jnp.concatenate([real, imag], 1))
        cos_part = left_mix(back_ref[0], field)
        sin_part = left_mix(back_ref[1], field)
        real = cos_part[:, :half] - sin_part[:, half:]
        imag = cos_part[:, half:] + sin_part[:, :half]
        out_ref[:, 0, 0, k] = real.reshape(group, rows, half).astype(out_ref.dtype)
        out_ref[:, 0, 1, k] = imag.reshape(group, rows, half).astype(out_ref.dtype)


def cross_spectra(first, turned, ref_turned, t):
    group, views, _, part, rows, half = turned.shape
    by = group * rows
    fwd, back = jnp.asarray(t["y_forward"]), jnp.asarray(t["y_back"])
    block = (group, 1, 2, 2, rows, half)
    return pl.pallas_call(
        functools.partial(cross_kernel, group * part),
        grid=(part // 2, views),
        out_shape=jax.ShapeDtypeStruct(turned.shape, F32),
        in_specs=[
            pl.BlockSpec(memory_space=pltpu.SMEM),
            pl.BlockSpec(block, lambda p, v: (0, v, 0, p, 0, 0)),
            pl.BlockSpec(block, lambda p, v: (0, 0, 0, p, 0, 0)),
            whole(fwd),
            whole(back),
        ],
        out_specs=pl.BlockSpec(block, lambda p, v: (0, v, 0, p, 0, 0)),
        scratch_shapes=[pltpu.VMEM((2, 4, by, half), F32)],
        compiler_params=params(),
        cost_estimate=cost(turned.size * 256 * 2 * 12, turned.size * 4, turned.size),
        name="cross_y",
    )(first, turned, ref_turned, fwd, back)


def inverse_kernel(back_ref, z_ref, x_ref, out_ref, held):
    group, _, _, part, rows, half = back_ref.shape
    depth = group * part
    for c in range(2):
        held[c] = back_ref[:, 0, c].astype(F32).reshape(depth, rows, half)
    for at in range(0, rows, SUB):
        real = held[0, :, at : at + SUB, :].reshape(depth * SUB, half)
        imag = held[1, :, at : at + SUB, :].reshape(depth * SUB, half)
        field = split(jnp.concatenate([real, imag], 1))
        cos_part = left_mix(z_ref[0], field)
        sin_part = left_mix(z_ref[1], field)
        real = cos_part[:, :half] - sin_part[:, half:]
        imag = cos_part[:, half:] + sin_part[:, :half]
        field = split(jnp.concatenate([real, imag], 1))
        result = right_mix(field, x_ref)
        out_ref[0, :, at : at + SUB, :] = result.reshape(depth, SUB, 2 * half)


def inverse_spectra(back, t):
    group, views, _, part, rows, half = back.shape
    depth = group * part
    shape = (views, depth, rows, 2 * half)
    z_table, x_table = jnp.asarray(t["z_back"]), jnp.asarray(t["x_back"])
    return pl.pallas_call(
        inverse_kernel,
        grid=(views,),
        out_shape=jax.ShapeDtypeStruct(shape, F32),
        in_specs=[
            pl.BlockSpec((group, 1) + back.shape[2:], lambda v: (0, v, 0, 0, 0, 0)),
            whole(z_table),
            whole(x_table),
        ],
        out_specs=pl.BlockSpec((1,) + shape[1:], lambda v: (v, 0, 0, 0)),
        scratch_shapes=[pltpu.VMEM((2, depth, rows, half), F32)],
        compiler_params=params(),
        cost_estimate=cost(back.size * 256 * 2 * 9, back.size * 6),
        name="surface_z_x",
    )(back, z_table, x_table)


def by_tap(taps, offsets):
    shape = (-1,) + (1,) * (offsets.ndim - 1)
    summed = jnp.zeros((taps.shape[0],) + offsets.shape[1:], F32)
    for i in range(TAPS):
        summed = jnp.where(offsets == i, taps[:, i].reshape(shape), summed)
    return summed


def blur_tables(filter_rows, shift_pairs, depth, width):
    size = depth * SUB
    at = jnp.arange(size, dtype=jnp.int32)
    row, col = at[:, None], at[None, :]
    z_off = (col // SUB - row // SUB + 7)[None]
    shift_z = shift_pairs[:, 0, None, None]
    block = jnp.arange(3, dtype=jnp.int32)[None, :, None, None]
    y_off = SUB * block + (col % SUB - row % SUB - SUB + 7)[None, None]
    z_forward = by_tap(filter_rows[:, 0], z_off - shift_z)
    z_back = by_tap(filter_rows[:, 0], 14 - z_off - shift_z)
    y_forward = by_tap(filter_rows[:, 1], y_off)
    y_back = by_tap(filter_rows[:, 1], 14 - y_off)
    zy_forward = (z_forward[:, None] * y_forward).astype(BF16)
    zy_back = (z_back[:, None] * y_back).astype(BF16)
    x_at = jnp.arange(width, dtype=jnp.int32)
    x_off = (x_at[:, None] - x_at[None, :] + 7)[None]
    shift_x = shift_pairs[:, 1, None, None]
    x_forward = by_tap(filter_rows[:, 2], x_off - shift_x)
    x_back = by_tap(filter_rows[:, 2], 14 - x_off - shift_x)
    return zy_forward, zy_back, jnp.stack(split(x_forward), 1), jnp.stack(split(x_back), 1)


def blur_blocks(blocks, zy_ref, x_ref, use):
    for b in range(len(blocks) - 2):
        total = None
        for j in range(3):
            for piece in blocks[b + j]:
                term = dot(zy_ref[0, j], piece)
                total = term if total is None else total + term
        use(b, right_mix(split(total), x_ref[0]))


def ratio_kernel(est_ref, low_ref, high_ref, obs_ref, zy_ref, x_ref, out_ref, head_ref, tail_ref, held):
    depth, rows, width = est_ref.shape
    count = rows // SUB
    held[...] = obs_ref[0].astype(F32)
    blocks = [(low_ref[...],)]
    for b in range(count):
        blocks.append(split(est_ref[:, b * SUB : (b + 1) * SUB, :].reshape(depth * SUB, width)))
    blocks.append((high_ref[...],))

    def use(b, blurred):
        seen = held[:, b * SUB : (b + 1) * SUB, :].reshape(depth * SUB, width)
        ratio = seen / blurred
        out_ref[0, b] = ratio
        if b == 0:
            head_ref[0] = ratio.astype(BF16)
        if b == count - 1:
            tail_ref[0] = ratio.astype(BF16)

    blur_blocks(blocks, zy_ref, x_ref, use)


def view_block(array):
    zeros = (0,) * (array.ndim - 1)
    return pl.BlockSpec((1,) + array.shape[1:], lambda v: (v,) + zeros)


def ratios(estimate, low, high, observed, zy, x_table):
    views, depth, rows, width = observed.shape
    size = depth * SUB
    outs = [
        jax.ShapeDtypeStruct((views, rows // SUB, size, width), F32),
        jax.ShapeDtypeStruct((views, size, width), BF16),
        jax.ShapeDtypeStruct((views, size, width), BF16),
    ]
    args = (estimate, low, high, observed, zy, x_table)
    return pl.pallas_call(
        ratio_kernel,
        grid=(views,),
        out_shape=outs,
        in_specs=[whole(a) for a in args[:3]] + [view_block(a) for a in args[3:]],
        out_specs=[view_block(a) for a in outs],
        scratch_shapes=[pltpu.VMEM((depth, rows, width), F32)],
        compiler_params=params(),
        cost_estimate=cost(observed.size * 256 * 2 * 9, observed.size * 8, observed.size),
        name="ratios",
    )(*args)


def update_kernel(ratio_ref, low_ref, high_ref, zy_ref, x_ref, out_ref):
    _, count, size, width = ratio_ref.shape
    depth = size // SUB
    blocks = [(low_ref[0],)]
    for b in range(count):
        blocks.append(split(ratio_ref[0, b]))
    blocks.append((high_ref[0],))
    first = pl.program_id(0) == 0

    def use(b, update):
        spot = (slice(None), slice(b * SUB, (b + 1) * SUB), slice(None))
        update = update.reshape(depth, SUB, width)
        out_ref[spot] = jnp.where(first, update, update * out_ref[spot])

    blur_blocks(blocks, zy_ref, x_ref, use)


def update_product(ratio, low, high, zy, x_table, shape):
    args = (ratio, low, high, zy, x_table)
    return pl.pallas_call(
        update_kernel,
        grid=(ratio.shape[0],),
        out_shape=jax.ShapeDtypeStruct(shape, F32),
        in_specs=[view_block(a) for a in args],
        out_specs=pl.BlockSpec(shape, lambda v: (0, 0, 0)),
        compiler_params=params(),
        cost_estimate=cost(ratio.size * 256 * 2 * 9, ratio.size * 6),
        name="updates",
    )(*args)


def from_sides(head, tail):
    count = lax.axis_size("gz")
    low = lax.ppermute(tail, "gz", [(i, i + 1) for i in range(count - 1)])
    high = lax.ppermute(head, "gz", [(i + 1, i) for i in range(count - 1)])
    return low, high


def from_partner(array):
    count = lax.axis_size("view")
    return lax.ppermute(array, "view", [(i, count - 1 - i) for i in range(count)])


def on_device(observed, initial, psf_taps, view_shifts, view_map):
    local_views = observed.shape[0]
    depth, rows, width = initial.shape
    gz = lax.axis_size("gz")
    t = tables(depth, rows * gz, width)
    group_index = lax.axis_index("view")
    slot_ids = group_index * local_views + jnp.arange(local_views, dtype=jnp.int32)
    all_slots = jnp.arange(view_map.shape[0], dtype=jnp.int32)
    chooser = slot_ids[:, None] == all_slots[None, :]
    view_ids = jnp.sum(jnp.where(chooser, view_map[None, :], 0), axis=1)
    picker = view_ids[:, None] == all_slots[None, :]
    filter_rows = jnp.sum(jnp.where(picker[:, :, None, None], psf_taps[None], 0.0), axis=1)
    shift_pairs = jnp.sum(jnp.where(picker[:, :, None], view_shifts[None, :, :], 0), axis=1)
    ref_slot = jnp.sum(jnp.where(view_map == 0, all_slots, 0))
    ref_group = ref_slot // local_views
    ref_local = ref_slot % local_views

    sent = forward_spectra(observed, gz, t)
    turned = lax.all_to_all(sent.astype(SENT), "gz", split_axis=0, concat_axis=0, tiled=True)
    turned = turned.astype(F32)
    mine = lax.dynamic_index_in_dim(turned, ref_local, 1, keepdims=True)
    ref_turned = jnp.where(group_index == ref_group, mine, from_partner(mine))
    first = (lax.axis_index("gz") == 0).astype(jnp.int32).reshape(1)
    crossed = cross_spectra(first, turned, ref_turned, t)
    back = lax.all_to_all(crossed.astype(SENT), "gz", split_axis=0, concat_axis=0, tiled=True)
    surfaces = inverse_spectra(back.astype(F32), t)

    zy_forward, zy_back, x_forward, x_back = blur_tables(filter_rows, shift_pairs, depth, width)
    size = depth * SUB
    estimate = initial
    for _ in range(ITERS):
        head = estimate[:, :SUB].astype(BF16).reshape(size, width)
        tail = estimate[:, rows - SUB :].astype(BF16).reshape(size, width)
        low, high = from_sides(head, tail)
        ratio, head, tail = ratios(estimate, low, high, observed, zy_forward, x_forward)
        low, high = from_sides(head, tail)
        product = update_product(ratio, low, high, zy_back, x_back, estimate.shape)
        product = product * from_partner(product)
        estimate = estimate * jnp.exp(jnp.log(product) / VIEWS)
    return estimate, surfaces


def solution(mesh):
    placed = (P("view", "parts", "gz", None), P("parts", "gz", None), P(), P(), P())
    return jax.shard_map(
        on_device,
        mesh=mesh,
        in_specs=placed,
        out_specs=(P("parts", "gz", None), P("view", "parts", "gz", None)),
        check_vma=False,
    )
```

```python
import functools
import math

import jax
import jax.numpy as jnp
import ml_dtypes
import numpy as np
from jax import lax
from jax.experimental import pallas as pl
from jax.experimental.pallas import tpu as pltpu
from jax.sharding import PartitionSpec as P

VIEWS = 8
BX = 256
ITERS = 2
TAPS = 15
SUB = 8
CENTRE = 1.1
F32 = jnp.float32
BF16 = jnp.bfloat16
SENT = jnp.float16
LIMIT = 56 * 1024 * 1024


def two(table):
    high = table.astype(ml_dtypes.bfloat16)
    low = (table - high.astype(np.float64)).astype(ml_dtypes.bfloat16)
    return np.stack([high, low])


def four(cosines, sines):
    pair = two(np.concatenate([cosines, sines], 0))
    return pair.reshape(-1, pair.shape[-1])


def depth_order(depth):
    order = [0, depth // 2]
    for k in range(1, depth // 2):
        order += [k, depth - k]
    return np.array(order)


def phase_tables(rows, columns, length):
    angles = 2.0 * math.pi / length * (np.outer(rows, columns) % length)
    return np.cos(angles), np.sin(angles)


@functools.lru_cache(None)
def tables(depth, by, bx):
    half = bx // 2
    norm = 1.0 / math.sqrt(depth * by * bx)
    c, s = phase_tables(np.arange(bx), np.arange(half), bx)
    alternate = 1.0 - 2.0 * (np.arange(bx) % 2)
    imag = -s
    imag[:, 0] = alternate
    x_forward = np.concatenate([c, imag], 1)
    weights = np.where(np.arange(half) == 0, 1.0, 2.0)
    imag = -s * weights
    imag[:, 0] = alternate
    x_back = np.concatenate([c * weights, imag], 1).T * norm
    zc, zs = phase_tables(depth_order(depth), np.arange(depth), depth)
    eye = np.eye(SUB)
    yc, ys = phase_tables(np.arange(by), np.arange(by), by)
    return dict(
        x_forward=two(x_forward),
        x_back=two(x_back),
        z_forward=four(np.kron(zc, eye), np.kron(zs, eye)),
        z_back=four(np.kron(zc.T, eye), np.kron(zs.T, eye)),
        y_forward=four(yc * norm, ys * norm),
        y_back=four(yc, ys),
    )


def dot(a, b):
    return jnp.dot(a, b, preferred_element_type=F32)


def split(a):
    high = a.astype(BF16)
    return high, (a - high.astype(F32)).astype(BF16)


def left_mix(table_ref, field):
    high, low = field
    size = table_ref.shape[0] // 4
    mixed = dot(table_ref[...], high)
    rest = dot(table_ref[: 2 * size], low)
    both = mixed[: 2 * size] + mixed[2 * size :] + rest
    return both[:size], both[size:]


def right_mix(field, table):
    high, low = field
    return dot(high, table[0]) + dot(low, table[0]) + dot(high, table[1])


def params():
    return pltpu.CompilerParams(vmem_limit_bytes=LIMIT)


def cost(flops, bytes_accessed, transcendentals=0):
    return pl.CostEstimate(
        flops=int(flops), bytes_accessed=int(bytes_accessed), transcendentals=int(transcendentals)
    )


def whole(array):
    zeros = (0,) * array.ndim
    return pl.BlockSpec(array.shape, lambda *_: zeros)


def forward_kernel(obs_ref, x_ref, z_ref, out_ref, held):
    _, depth, rows, width = obs_ref.shape
    half = width // 2
    group, _, _, part, _, _ = out_ref.shape
    lane = lax.broadcasted_iota(jnp.int32, (1, width), 1)
    centre = jnp.where(lane == 0, CENTRE * width, 0.0).astype(F32)
    flat = obs_ref[0].reshape(depth * rows, width)
    mixed = dot(flat, x_ref[0]) + dot(flat, x_ref[1]) - centre
    mixed = mixed.reshape(depth, rows, width)
    for at in range(0, rows, SUB):
        field = split(mixed[:, at : at + SUB, :].reshape(depth * SUB, width))
        cos_part, sin_part = left_mix(z_ref, field)
        real = cos_part[:, :half] + sin_part[:, half:]
        imag = cos_part[:, half:] - sin_part[:, :half]
        held[0, :, at : at + SUB, :] = real.reshape(depth, SUB, half)
        held[1, :, at : at + SUB, :] = imag.reshape(depth, SUB, half)
    for c in range(2):
        out_ref[:, 0, c] = held[c].reshape(group, part, rows, half).astype(out_ref.dtype)


def forward_spectra(observed, group, t):
    views, depth, rows, width = observed.shape
    part = depth // group
    shape = (group, views, 2, part, rows, width // 2)
    x_table, z_table = jnp.asarray(t["x_forward"]), jnp.asarray(t["z_forward"])
    return pl.pallas_call(
        forward_kernel,
        grid=(views,),
        out_shape=jax.ShapeDtypeStruct(shape, F32),
        in_specs=[
            pl.BlockSpec((1,) + observed.shape[1:], lambda v: (v, 0, 0, 0)),
            whole(x_table),
            whole(z_table),
        ],
        out_specs=pl.BlockSpec((group, 1) + shape[2:], lambda v: (0, v, 0, 0, 0, 0)),
        scratch_shapes=[pltpu.VMEM((2, depth, rows, width // 2), F32)],
        compiler_params=params(),
        cost_estimate=cost(observed.size * 256 * 2 * 8, observed.size * 4),
        name="spectra_x_z",
    )(observed, x_table, z_table)


def cross_kernel(depth, first_ref, spec_ref, ref_ref, fwd_ref, back_ref, out_ref, held):
    group, _, _, _, rows, half = spec_ref.shape
    by = group * rows
    pair = pl.program_id(0)
    alone = jnp.logical_and(first_ref[0] == 1, pair == 0)
    lane0 = lax.broadcasted_iota(jnp.int32, (by, half), 1) == 0
    row0 = lax.broadcasted_iota(jnp.int32, (by, half), 0) == 0
    total = CENTRE * math.sqrt(depth * by * 2 * half)
    origin = jnp.logical_and(lane0, row0)

    def spectrum(ref):
        straight, turned = [], []
        for k in range(2):
            real = ref[:, 0, 0, k].astype(F32).reshape(by, half)
            imag = ref[:, 0, 1, k].astype(F32).reshape(by, half)
            field = split(jnp.concatenate([real, imag], 1))
            cos_part, sin_part = left_mix(fwd_ref, field)
            cos_real = cos_part[:, :half]
            if k == 0:
                cos_real = cos_real + jnp.where(jnp.logical_and(origin, alone), total, 0.0)
            straight.append((cos_real + sin_part[:, half:], cos_part[:, half:] - sin_part[:, :half]))
            turned.append((cos_real - sin_part[:, half:], cos_part[:, half:] + sin_part[:, :half]))
        out = []
        for k in range(2):
            real, imag = straight[k]
            other_real = jnp.where(alone, turned[k][0], turned[1 - k][0])
            other_imag = jnp.where(alone, turned[k][1], turned[1 - k][1])
            out.append(
                (
                    jnp.where(lane0, 0.5 * (real + other_real), real),
                    jnp.where(lane0, 0.5 * (imag - other_imag), imag),
                    0.5 * (imag + other_imag),
                    0.5 * (other_real - real),
                )
            )
        return out

    @pl.when(pl.program_id(1) == 0)
    def _():
        for k, member in enumerate(spectrum(ref_ref)):
            for i in range(4):
                held[k, i] = member[i]

    def cross(sr, si, rr, ri):
        magnitude = jnp.sqrt((sr * sr + si * si) * (rr * rr + ri * ri))
        scale = 1.0 / (magnitude + 1.0)
        return (sr * rr + si * ri) * scale, (si * rr - sr * ri) * scale

    for k, member in enumerate(spectrum(spec_ref)):
        real, imag = cross(member[0], member[1], held[k, 0], held[k, 1])
        top_real, top_imag = cross(member[2], member[3], held[k, 2], held[k, 3])
        real = jnp.where(lane0, real - top_imag, real)
        imag = jnp.where(lane0, imag + top_real, imag)
        field = split(jnp.concatenate([real, imag], 1))
        cos_part, sin_part = left_mix(back_ref, field)
        real = cos_part[:, :half] - sin_part[:, half:]
        imag = cos_part[:, half:] + sin_part[:, :half]
        out_ref[:, 0, 0, k] = real.reshape(group, rows, half).astype(out_ref.dtype)
        out_ref[:, 0, 1, k] = imag.reshape(group, rows, half).astype(out_ref.dtype)


def cross_spectra(first, turned, ref_turned, t):
    group, views, _, part, rows, half = turned.shape
    by = group * rows
    fwd, back = jnp.asarray(t["y_forward"]), jnp.asarray(t["y_back"])
    block = (group, 1, 2, 2, rows, half)
    return pl.pallas_call(
        functools.partial(cross_kernel, group * part),
        grid=(part // 2, views),
        out_shape=jax.ShapeDtypeStruct(turned.shape, F32),
        in_specs=[
            pl.BlockSpec(memory_space=pltpu.SMEM),
            pl.BlockSpec(block, lambda p, v: (0, v, 0, p, 0, 0)),
            pl.BlockSpec(block, lambda p, v: (0, 0, 0, p, 0, 0)),
            whole(fwd),
            whole(back),
        ],
        out_specs=pl.BlockSpec(block, lambda p, v: (0, v, 0, p, 0, 0)),
        scratch_shapes=[pltpu.VMEM((2, 4, by, half), F32)],
        compiler_params=params(),
        cost_estimate=cost(turned.size * 256 * 2 * 12, turned.size * 4, turned.size),
        name="cross_y",
    )(first, turned, ref_turned, fwd, back)


def inverse_kernel(back_ref, z_ref, x_ref, out_ref, held):
    group, _, _, part, rows, half = back_ref.shape
    depth = group * part
    for c in range(2):
        held[c] = back_ref[:, 0, c].astype(F32).reshape(depth, rows, half)
    for at in range(0, rows, SUB):
        real = held[0, :, at : at + SUB, :].reshape(depth * SUB, half)
        imag = held[1, :, at : at + SUB, :].reshape(depth * SUB, half)
        field = split(jnp.concatenate([real, imag], 1))
        cos_part, sin_part = left_mix(z_ref, field)
        real = cos_part[:, :half] - sin_part[:, half:]
        imag = cos_part[:, half:] + sin_part[:, :half]
        field = split(jnp.concatenate([real, imag], 1))
        result = right_mix(field, x_ref)
        out_ref[0, :, at : at + SUB, :] = result.reshape(depth, SUB, 2 * half)


def inverse_spectra(back, t):
    group, views, _, part, rows, half = back.shape
    depth = group * part
    shape = (views, depth, rows, 2 * half)
    z_table, x_table = jnp.asarray(t["z_back"]), jnp.asarray(t["x_back"])
    return pl.pallas_call(
        inverse_kernel,
        grid=(views,),
        out_shape=jax.ShapeDtypeStruct(shape, F32),
        in_specs=[
            pl.BlockSpec((group, 1) + back.shape[2:], lambda v: (0, v, 0, 0, 0, 0)),
            whole(z_table),
            whole(x_table),
        ],
        out_specs=pl.BlockSpec((1,) + shape[1:], lambda v: (v, 0, 0, 0)),
        scratch_shapes=[pltpu.VMEM((2, depth, rows, half), F32)],
        compiler_params=params(),
        cost_estimate=cost(back.size * 256 * 2 * 9, back.size * 6),
        name="surface_z_x",
    )(back, z_table, x_table)


def by_tap(row, offsets):
    summed = jnp.zeros(offsets.shape, F32)
    for i in range(TAPS):
        summed = jnp.where(offsets == i, row(i), summed)
    return summed


def table_kernel(depth, group_ref, map_ref, shift_ref, taps_ref, zyf_ref, zyb_ref, xf_ref, xb_ref):
    width = xf_ref.shape[-1]
    size = depth * SUB
    view = map_ref[group_ref[0] * pl.num_programs(0) + pl.program_id(0)]
    shift_z, shift_x = shift_ref[view, 0], shift_ref[view, 1]

    def taps(axis):
        return lambda i: taps_ref[view, axis * TAPS + i]

    def places(rows, columns):
        shape = (rows, columns)
        return [lax.broadcasted_iota(jnp.int32, shape, d) for d in range(2)]

    row, col = places(depth, size)
    z_off = lax.shift_right_logical(col, 3) - row + 7
    z_pair = by_tap(taps(0), z_off - shift_z), by_tap(taps(0), 14 - z_off - shift_z)
    row, col = places(SUB, size)
    for j in range(3):
        y_off = SUB * (j - 1) + jnp.bitwise_and(col, SUB - 1) - row + 7
        y_pair = by_tap(taps(1), y_off), by_tap(taps(1), 14 - y_off)
        for ref, z, y in zip((zyf_ref, zyb_ref), z_pair, y_pair):
            both = (z[:, None, :] * y[None]).reshape(size, size)
            ref[0, j * size : (j + 1) * size] = both.astype(BF16)
    row, col = places(width, width)
    x_off = row - col + 7
    xf_ref[0] = by_tap(taps(2), x_off - shift_x).astype(BF16)
    xb_ref[0] = by_tap(taps(2), 14 - x_off - shift_x).astype(BF16)


def view_block(array):
    zeros = (0,) * (array.ndim - 1)
    return pl.BlockSpec((1,) + array.shape[1:], lambda v: (v,) + zeros)


def blur_tables(group_index, view_map, view_shifts, psf_taps, views, depth, width):
    size = depth * SUB
    zy = jax.ShapeDtypeStruct((views, 3 * size, size), BF16)
    x = jax.ShapeDtypeStruct((views, width, width), BF16)
    return pl.pallas_call(
        functools.partial(table_kernel, depth),
        grid=(views,),
        out_shape=[zy, zy, x, x],
        in_specs=[pl.BlockSpec(memory_space=pltpu.SMEM)] * 4,
        out_specs=[view_block(zy), view_block(zy), view_block(x), view_block(x)],
        compiler_params=params(),
        cost_estimate=cost(views * size * size * 100, views * size * size * 16),
        name="blur_tables",
    )(group_index.reshape(1), view_map, view_shifts, psf_taps.reshape(psf_taps.shape[0], -1))


def blur(pieces, zy_ref, x_ref, total, use):
    count = len(pieces) - 2
    size = zy_ref.shape[2]
    for b, piece in enumerate(pieces):
        steps = [j for j in range(3) if 0 <= b - j < count]
        table = zy_ref[0, steps[0] * size : (steps[-1] + 1) * size]
        mixed = dot(table, piece[0])
        for part in piece[1:]:
            mixed = mixed + dot(table, part)
        for j in steps:
            part = mixed[(j - steps[0]) * size : (j - steps[0] + 1) * size]
            if j == 0:
                total[b - j] = part
            elif j == 1:
                total[b - j] += part
            else:
                done = dot(jnp.concatenate(split(total[b - j] + part), 0), x_ref[0])
                use(b - j, done[:size] + done[size:])


def join_kernel(
    est_ref, low_ref, high_ref, obs_ref, obs_low_ref, obs_high_ref,
    zyf_ref, zyb_ref, xf_ref, xb_ref, out_ref, held, total, ratio,
):
    depth, rows, width = est_ref.shape
    size = depth * SUB
    count = rows // SUB
    held[...] = obs_ref[0].astype(F32)
    pieces = [(low_ref[0],), (low_ref[1],)]
    for b in range(count):
        pieces.append(split(est_ref[:, b * SUB : (b + 1) * SUB, :].reshape(size, width)))
    pieces += [(high_ref[0],), (high_ref[1],)]

    def keep_ratio(b, blurred):
        if b == 0:
            seen = obs_low_ref[0].astype(F32)
        elif b == count + 1:
            seen = obs_high_ref[0].astype(F32)
        else:
            seen = held[:, (b - 1) * SUB : b * SUB, :].reshape(size, width)
        value = seen / blurred
        if b in (0, count + 1):
            value = jnp.where(seen > 0.0, value, 0.0)
        ratio[b, 0], ratio[b, 1] = split(value)

    blur(pieces, zyf_ref, xf_ref, total, keep_ratio)
    first = pl.program_id(0) == 0

    def keep_update(b, update):
        spot = (slice(None), slice(b * SUB, (b + 1) * SUB), slice(None))
        update = update.reshape(depth, SUB, width)
        out_ref[spot] = jnp.where(first, update, update * out_ref[spot])

    pieces = [(ratio[b, 0], ratio[b, 1]) for b in range(count + 2)]
    blur(pieces, zyb_ref, xb_ref, total, keep_update)


def join_views(estimate, low, high, observed, obs_low, obs_high, blurs):
    depth, rows, width = estimate.shape
    size = depth * SUB
    count = rows // SUB
    args = (estimate, low, high, observed, obs_low, obs_high) + tuple(blurs)
    return pl.pallas_call(
        join_kernel,
        grid=(observed.shape[0],),
        out_shape=jax.ShapeDtypeStruct(estimate.shape, F32),
        in_specs=[whole(a) for a in args[:3]] + [view_block(a) for a in args[3:]],
        out_specs=whole(estimate),
        scratch_shapes=[
            pltpu.VMEM((depth, rows, width), F32),
            pltpu.VMEM((count + 2, size, width), F32),
            pltpu.VMEM((count + 2, 2, size, width), BF16),
        ],
        compiler_params=params(),
        cost_estimate=cost(observed.size * 256 * 2 * 20, observed.size * 8, observed.size),
        name="join_views",
    )(*args)


def blocks_of(rows_of, depth, count, width):
    shape = rows_of.shape[:-3]
    split_up = rows_of.astype(BF16).reshape(shape + (depth, count, SUB, width))
    return jnp.swapaxes(split_up, -4, -3).reshape(shape + (count, depth * SUB, width))


def from_sides(head, tail):
    count = lax.axis_size("gz")
    low = lax.ppermute(tail, "gz", [(i, i + 1) for i in range(count - 1)])
    high = lax.ppermute(head, "gz", [(i + 1, i) for i in range(count - 1)])
    return low, high


def from_partner(array):
    count = lax.axis_size("view")
    return lax.ppermute(array, "view", [(i, count - 1 - i) for i in range(count)])


def on_device(observed, initial, psf_taps, view_shifts, view_map):
    local_views = observed.shape[0]
    depth, rows, width = initial.shape
    gz = lax.axis_size("gz")
    t = tables(depth, rows * gz, width)
    group_index = lax.axis_index("view")
    all_slots = jnp.arange(view_map.shape[0], dtype=jnp.int32)
    ref_slot = jnp.sum(jnp.where(view_map == 0, all_slots, 0))
    ref_group = ref_slot // local_views
    ref_local = ref_slot % local_views

    def est_sides(estimate):
        head = blocks_of(estimate[:, : 2 * SUB], depth, 2, width)
        tail = blocks_of(estimate[:, rows - 2 * SUB :], depth, 2, width)
        return from_sides(head, tail)

    obs_sides = from_sides(
        blocks_of(observed[:, :, :SUB], depth, 1, width)[:, 0],
        blocks_of(observed[:, :, rows - SUB :], depth, 1, width)[:, 0],
    )
    sides = est_sides(initial)
    blurs = blur_tables(group_index, view_map, view_shifts, psf_taps, local_views, depth, width)

    def joined(estimate, sides):
        product = join_views(estimate, *sides, observed, *obs_sides, blurs)
        product = product * from_partner(product)
        return estimate * jnp.exp(jnp.log(product) / VIEWS)

    sent = forward_spectra(observed, gz, t).astype(SENT)
    turned = lax.all_to_all(sent, "gz", split_axis=0, concat_axis=0, tiled=True)
    estimate = joined(initial, sides)

    turned, estimate = lax.optimization_barrier((turned, estimate))
    sides = est_sides(estimate)
    mine = lax.dynamic_index_in_dim(turned, ref_local, 1, keepdims=True)
    ref_turned = jnp.where(group_index == ref_group, mine, from_partner(mine)).astype(F32)
    first = (lax.axis_index("gz") == 0).astype(jnp.int32).reshape(1)
    crossed = cross_spectra(first, turned.astype(F32), ref_turned, t).astype(SENT)
    crossed, sides = lax.optimization_barrier((crossed, sides))
    back = lax.all_to_all(crossed, "gz", split_axis=0, concat_axis=0, tiled=True)
    for step in range(1, ITERS):
        if step > 1:
            sides = est_sides(estimate)
        estimate = joined(estimate, sides)
    surfaces = inverse_spectra(back.astype(F32), t)
    return estimate, surfaces


def solution(mesh):
    placed = (P("view", "parts", "gz", None), P("parts", "gz", None), P(), P(), P())
    return jax.shard_map(
        on_device,
        mesh=mesh,
        in_specs=placed,
        out_specs=(P("parts", "gz", None), P("view", "parts", "gz", None)),
        check_vma=False,
    )
```

```python
import functools
import math

import jax
import jax.numpy as jnp
import ml_dtypes
import numpy as np
from jax import lax
from jax.experimental import pallas as pl
from jax.experimental.pallas import tpu as pltpu
from jax.sharding import PartitionSpec as P

VIEWS = 8
BX = 256
ITERS = 2
TAPS = 15
SUB = 8
CENTRE = 1.1
F32 = jnp.float32
BF16 = jnp.bfloat16
SENT = jnp.float16
LIMIT = 56 * 1024 * 1024


def two(table):
    high = table.astype(ml_dtypes.bfloat16)
    low = (table - high.astype(np.float64)).astype(ml_dtypes.bfloat16)
    return np.stack([high, low])


def left_table(cosines, sines):
    high, low = two(np.concatenate([cosines, sines], 0))
    return np.concatenate([high, low, high], 1)


def right_table(table):
    high, low = two(table)
    return np.concatenate([high, high, low], 0)


def depth_order(depth):
    order = [0, depth // 2]
    for k in range(1, depth // 2):
        order += [k, depth - k]
    return np.array(order)


def phase_tables(rows, columns, length):
    angles = 2.0 * math.pi / length * (np.outer(rows, columns) % length)
    return np.cos(angles), np.sin(angles)


@functools.lru_cache(None)
def tables(depth, by, bx):
    half = bx // 2
    norm = 1.0 / math.sqrt(depth * by * bx)
    c, s = phase_tables(np.arange(bx), np.arange(half), bx)
    alternate = 1.0 - 2.0 * (np.arange(bx) % 2)
    imag = -s
    imag[:, 0] = alternate
    x_forward = np.concatenate([c, imag], 1)
    weights = np.where(np.arange(half) == 0, 1.0, 2.0)
    imag = -s * weights
    imag[:, 0] = alternate
    x_back = np.concatenate([c * weights, imag], 1).T * norm
    zc, zs = phase_tables(depth_order(depth), np.arange(depth), depth)
    eye = np.eye(SUB)
    yc, ys = phase_tables(np.arange(by), np.arange(by), by)
    return dict(
        x_forward=two(x_forward).reshape(2 * bx, bx),
        x_back=right_table(x_back),
        z_forward=left_table(np.kron(zc, eye), np.kron(zs, eye)),
        z_back=left_table(np.kron(zc.T, eye), np.kron(zs.T, eye)),
        y_forward=left_table(yc * norm, ys * norm),
        y_back=left_table(yc, ys),
    )


def dot(a, b):
    return jnp.dot(a, b, preferred_element_type=F32)


def split(a):
    high = a.astype(BF16)
    return high, (a - high.astype(F32)).astype(BF16)


def left_mix(table_ref, field):
    high, low = field
    both = dot(table_ref[...], jnp.concatenate([high, high, low], 0))
    size = table_ref.shape[0] // 2
    return both[:size], both[size:]


def right_mix(field, table_ref):
    high, low = field
    return dot(jnp.concatenate([high, low, high], 1), table_ref[...])


def params():
    return pltpu.CompilerParams(vmem_limit_bytes=LIMIT)


def cost(flops, bytes_accessed, transcendentals=0):
    return pl.CostEstimate(
        flops=int(flops), bytes_accessed=int(bytes_accessed), transcendentals=int(transcendentals)
    )


def whole(array):
    zeros = (0,) * array.ndim
    return pl.BlockSpec(array.shape, lambda *_: zeros)


def forward_kernel(obs_ref, x_ref, z_ref, *rest):
    out_refs, held = rest[:-1], rest[-1]
    _, depth, rows, width = obs_ref.shape
    half = width // 2
    group = out_refs[0].shape[0]
    lane = lax.broadcasted_iota(jnp.int32, (1, width), 1)
    centre = jnp.where(lane == 0, CENTRE * width, 0.0).astype(F32)
    flat = obs_ref[0].reshape(depth * rows, width)
    mixed = dot(jnp.concatenate([flat, flat], 1), x_ref[...]) - centre
    mixed = mixed.reshape(depth, rows, width)
    for at in range(0, rows, SUB):
        field = split(mixed[:, at : at + SUB, :].reshape(depth * SUB, width))
        cos_part, sin_part = left_mix(z_ref, field)
        real = cos_part[:, :half] + sin_part[:, half:]
        imag = cos_part[:, half:] - sin_part[:, :half]
        held[0, :, at : at + SUB, :] = real.reshape(depth, SUB, half)
        held[1, :, at : at + SUB, :] = imag.reshape(depth, SUB, half)
    for c in range(2):
        field = held[c].reshape(group, depth // group, rows, half)
        for p, out_ref in enumerate(out_refs):
            out_ref[:, 0, c] = field[:, 2 * p : 2 * p + 2]


def forward_spectra(observed, group, t):
    views, depth, rows, width = observed.shape
    chunks = depth // group // 2
    shape = (group, views, 2, 2, rows, width // 2)
    x_table, z_table = jnp.asarray(t["x_forward"]), jnp.asarray(t["z_forward"])
    return pl.pallas_call(
        forward_kernel,
        grid=(views,),
        out_shape=[jax.ShapeDtypeStruct(shape, F32)] * chunks,
        in_specs=[
            pl.BlockSpec((1,) + observed.shape[1:], lambda v: (v, 0, 0, 0)),
            whole(x_table),
            whole(z_table),
        ],
        out_specs=[pl.BlockSpec((group, 1) + shape[2:], lambda v: (0, v, 0, 0, 0, 0))] * chunks,
        scratch_shapes=[pltpu.VMEM((2, depth, rows, width // 2), F32)],
        compiler_params=params(),
        cost_estimate=cost(observed.size * 256 * 2 * 8, observed.size * 4),
        name="spectra_x_z",
    )(observed, x_table, z_table)


def cross_kernel(depth, first_ref, spec_ref, ref_ref, fwd_ref, back_ref, out_ref, held):
    group, _, _, _, rows, half = spec_ref.shape
    by = group * rows
    alone = first_ref[0] == 1
    lane0 = lax.broadcasted_iota(jnp.int32, (by, half), 1) == 0
    row0 = lax.broadcasted_iota(jnp.int32, (by, half), 0) == 0
    total = CENTRE * math.sqrt(depth * by * 2 * half)
    origin = jnp.logical_and(lane0, row0)

    def spectrum(ref):
        straight, turned = [], []
        for k in range(2):
            real = ref[:, 0, 0, k].astype(F32).reshape(by, half)
            imag = ref[:, 0, 1, k].astype(F32).reshape(by, half)
            field = split(jnp.concatenate([real, imag], 1))
            cos_part, sin_part = left_mix(fwd_ref, field)
            cos_real = cos_part[:, :half]
            if k == 0:
                cos_real = cos_real + jnp.where(jnp.logical_and(origin, alone), total, 0.0)
            straight.append((cos_real + sin_part[:, half:], cos_part[:, half:] - sin_part[:, :half]))
            turned.append((cos_real - sin_part[:, half:], cos_part[:, half:] + sin_part[:, :half]))
        out = []
        for k in range(2):
            real, imag = straight[k]
            other_real = jnp.where(alone, turned[k][0], turned[1 - k][0])
            other_imag = jnp.where(alone, turned[k][1], turned[1 - k][1])
            out.append(
                (
                    jnp.where(lane0, 0.5 * (real + other_real), real),
                    jnp.where(lane0, 0.5 * (imag - other_imag), imag),
                    0.5 * (imag + other_imag),
                    0.5 * (other_real - real),
                )
            )
        return out

    @pl.when(pl.program_id(0) == 0)
    def _():
        for k, member in enumerate(spectrum(ref_ref)):
            for i in range(4):
                held[k, i] = member[i]

    def cross(sr, si, rr, ri):
        magnitude = jnp.sqrt((sr * sr + si * si) * (rr * rr + ri * ri))
        scale = 1.0 / (magnitude + 1.0)
        return (sr * rr + si * ri) * scale, (si * rr - sr * ri) * scale

    for k, member in enumerate(spectrum(spec_ref)):
        real, imag = cross(member[0], member[1], held[k, 0], held[k, 1])
        top_real, top_imag = cross(member[2], member[3], held[k, 2], held[k, 3])
        real = jnp.where(lane0, real - top_imag, real)
        imag = jnp.where(lane0, imag + top_real, imag)
        field = split(jnp.concatenate([real, imag], 1))
        cos_part, sin_part = left_mix(back_ref, field)
        real = cos_part[:, :half] - sin_part[:, half:]
        imag = cos_part[:, half:] + sin_part[:, :half]
        out_ref[:, 0, 0, k] = real.reshape(group, rows, half).astype(out_ref.dtype)
        out_ref[:, 0, 1, k] = imag.reshape(group, rows, half).astype(out_ref.dtype)


def cross_spectra(first, depth, turned, ref_turned, t):
    group, views, _, _, rows, half = turned.shape
    by = group * rows
    fwd, back = jnp.asarray(t["y_forward"]), jnp.asarray(t["y_back"])
    block = (group, 1, 2, 2, rows, half)
    return pl.pallas_call(
        functools.partial(cross_kernel, depth),
        grid=(views,),
        out_shape=jax.ShapeDtypeStruct(turned.shape, F32),
        in_specs=[
            pl.BlockSpec(memory_space=pltpu.SMEM),
            pl.BlockSpec(block, lambda v: (0, v, 0, 0, 0, 0)),
            pl.BlockSpec(block, lambda v: (0, 0, 0, 0, 0, 0)),
            whole(fwd),
            whole(back),
        ],
        out_specs=pl.BlockSpec(block, lambda v: (0, v, 0, 0, 0, 0)),
        scratch_shapes=[pltpu.VMEM((2, 4, by, half), F32)],
        compiler_params=params(),
        cost_estimate=cost(turned.size * 256 * 2 * 12, turned.size * 4, turned.size),
        name="cross_y",
    )(first, turned, ref_turned, fwd, back)


def inverse_kernel(*refs):
    back_refs, (z_ref, x_ref, out_ref, held) = refs[:-4], refs[-4:]
    group, _, _, _, rows, half = back_refs[0].shape
    depth = group * 2 * len(back_refs)
    for c in range(2):
        field = jnp.concatenate([ref[:, 0, c] for ref in back_refs], 1)
        held[c] = field.reshape(depth, rows, half)
    for at in range(0, rows, SUB):
        real = held[0, :, at : at + SUB, :].reshape(depth * SUB, half)
        imag = held[1, :, at : at + SUB, :].reshape(depth * SUB, half)
        field = split(jnp.concatenate([real, imag], 1))
        cos_part, sin_part = left_mix(z_ref, field)
        real = cos_part[:, :half] - sin_part[:, half:]
        imag = cos_part[:, half:] + sin_part[:, :half]
        field = split(jnp.concatenate([real, imag], 1))
        result = right_mix(field, x_ref)
        out_ref[0, :, at : at + SUB, :] = result.reshape(depth, SUB, 2 * half)


def inverse_spectra(backs, t):
    group, views, _, _, rows, half = backs[0].shape
    depth = group * 2 * len(backs)
    shape = (views, depth, rows, 2 * half)
    z_table, x_table = jnp.asarray(t["z_back"]), jnp.asarray(t["x_back"])
    return pl.pallas_call(
        inverse_kernel,
        grid=(views,),
        out_shape=jax.ShapeDtypeStruct(shape, F32),
        in_specs=[
            *[pl.BlockSpec((group, 1) + b.shape[2:], lambda v: (0, v, 0, 0, 0, 0)) for b in backs],
            whole(z_table),
            whole(x_table),
        ],
        out_specs=pl.BlockSpec((1,) + shape[1:], lambda v: (v, 0, 0, 0)),
        scratch_shapes=[pltpu.VMEM((2, depth, rows, half), F32)],
        compiler_params=params(),
        cost_estimate=cost(math.prod(shape) * 256 * 2 * 9, math.prod(shape) * 8),
        name="surface_z_x",
    )(*backs, z_table, x_table)


def by_tap(row, offsets):
    summed = jnp.zeros(offsets.shape, F32)
    for i in range(TAPS):
        summed = jnp.where(offsets == i, row(i), summed)
    return summed


def table_kernel(depth, group_ref, map_ref, shift_ref, taps_ref, zyf_ref, zyb_ref, xf_ref, xb_ref):
    width = xf_ref.shape[-1]
    size = depth * SUB
    view = map_ref[group_ref[0] * pl.num_programs(0) + pl.program_id(0)]
    shift_z, shift_x = shift_ref[view, 0], shift_ref[view, 1]

    def taps(axis):
        return lambda i: taps_ref[view, axis * TAPS + i]

    def places(rows, columns):
        shape = (rows, columns)
        return [lax.broadcasted_iota(jnp.int32, shape, d) for d in range(2)]

    row, col = places(depth, size)
    z_off = lax.shift_right_logical(col, 3) - row + 7
    z_pair = by_tap(taps(0), z_off - shift_z), by_tap(taps(0), 14 - z_off - shift_z)
    row, col = places(SUB, size)
    for j in range(3):
        y_off = SUB * (j - 1) + jnp.bitwise_and(col, SUB - 1) - row + 7
        y_pair = by_tap(taps(1), y_off), by_tap(taps(1), 14 - y_off)
        for ref, z, y in zip((zyf_ref, zyb_ref), z_pair, y_pair):
            both = (z[:, None, :] * y[None]).reshape(size, size)
            ref[0, j * size : (j + 1) * size] = both.astype(BF16)
    row, col = places(width, width)
    x_off = row - col + 7
    xf_ref[0] = by_tap(taps(2), x_off - shift_x).astype(BF16)
    xb_ref[0] = by_tap(taps(2), 14 - x_off - shift_x).astype(BF16)


def view_block(array):
    zeros = (0,) * (array.ndim - 1)
    return pl.BlockSpec((1,) + array.shape[1:], lambda v: (v,) + zeros)


def blur_tables(group_index, view_map, view_shifts, psf_taps, views, depth, width):
    size = depth * SUB
    zy = jax.ShapeDtypeStruct((views, 3 * size, size), BF16)
    x = jax.ShapeDtypeStruct((views, width, width), BF16)
    return pl.pallas_call(
        functools.partial(table_kernel, depth),
        grid=(views,),
        out_shape=[zy, zy, x, x],
        in_specs=[pl.BlockSpec(memory_space=pltpu.SMEM)] * 4,
        out_specs=[view_block(zy), view_block(zy), view_block(x), view_block(x)],
        compiler_params=params(),
        cost_estimate=cost(views * size * size * 100, views * size * size * 16),
        name="blur_tables",
    )(group_index.reshape(1), view_map, view_shifts, psf_taps.reshape(psf_taps.shape[0], -1))


def blur(pieces, zy_ref, x_ref, total, use):
    count = len(pieces) - 2
    size = zy_ref.shape[2]
    for b, piece in enumerate(pieces):
        steps = [j for j in range(3) if 0 <= b - j < count]
        table = zy_ref[0, steps[0] * size : (steps[-1] + 1) * size]
        table = jnp.concatenate([table] * len(piece), 1)
        mixed = dot(table, jnp.concatenate(piece, 0) if len(piece) > 1 else piece[0])
        for j in steps:
            part = mixed[(j - steps[0]) * size : (j - steps[0] + 1) * size]
            if j == 0:
                total[b - j] = part
            elif j == 1:
                total[b - j] += part
            else:
                done = dot(jnp.concatenate(split(total[b - j] + part), 0), x_ref[0])
                use(b - j, done[:size] + done[size:])


def join_kernel(
    est_ref, low_ref, high_ref, obs_ref, obs_low_ref, obs_high_ref,
    zyf_ref, zyb_ref, xf_ref, xb_ref, out_ref, held, total, ratio,
):
    depth, rows, width = est_ref.shape
    size = depth * SUB
    count = rows // SUB
    held[...] = obs_ref[0].astype(F32)
    pieces = [(low_ref[0],), (low_ref[1],)]
    for b in range(count):
        pieces.append(split(est_ref[:, b * SUB : (b + 1) * SUB, :].reshape(size, width)))
    pieces += [(high_ref[0],), (high_ref[1],)]

    def keep_ratio(b, blurred):
        if b == 0:
            seen = obs_low_ref[0].astype(F32)
        elif b == count + 1:
            seen = obs_high_ref[0].astype(F32)
        else:
            seen = held[:, (b - 1) * SUB : b * SUB, :].reshape(size, width)
        value = seen / blurred
        if b in (0, count + 1):
            value = jnp.where(seen > 0.0, value, 0.0)
        ratio[b, 0], ratio[b, 1] = split(value)

    blur(pieces, zyf_ref, xf_ref, total, keep_ratio)
    first = pl.program_id(0) == 0

    def keep_update(b, update):
        spot = (slice(None), slice(b * SUB, (b + 1) * SUB), slice(None))
        update = update.reshape(depth, SUB, width)
        out_ref[spot] = jnp.where(first, update, update * out_ref[spot])

    pieces = [(ratio[b, 0], ratio[b, 1]) for b in range(count + 2)]
    blur(pieces, zyb_ref, xb_ref, total, keep_update)


def join_views(estimate, sides, observed, obs_sides, blurs):
    depth, rows, width = estimate.shape
    size = depth * SUB
    count = rows // SUB
    args = (estimate,) + tuple(sides) + (observed,) + tuple(obs_sides) + tuple(blurs)
    side = pl.BlockSpec((2, size, width), lambda v: (0, 0, 0))
    obs_side = pl.BlockSpec((1, size, width), lambda v: (v + 2, 0, 0))
    return pl.pallas_call(
        join_kernel,
        grid=(observed.shape[0],),
        out_shape=jax.ShapeDtypeStruct(estimate.shape, F32),
        in_specs=[whole(estimate), side, side, view_block(observed), obs_side, obs_side]
        + [view_block(a) for a in blurs],
        out_specs=whole(estimate),
        scratch_shapes=[
            pltpu.VMEM((depth, rows, width), F32),
            pltpu.VMEM((count + 2, size, width), F32),
            pltpu.VMEM((count + 2, 2, size, width), BF16),
        ],
        compiler_params=params(),
        cost_estimate=cost(observed.size * 256 * 2 * 20, observed.size * 8, observed.size),
        name="join_views",
    )(*args)


def blocks_of(rows_of, depth, count, width):
    shape = rows_of.shape[:-3]
    split_up = rows_of.astype(BF16).reshape(shape + (depth, count, SUB, width))
    return jnp.swapaxes(split_up, -4, -3).reshape(shape + (count, depth * SUB, width))


def from_sides(head, tail):
    count = lax.axis_size("gz")
    low = lax.ppermute(tail, "gz", [(i, i + 1) for i in range(count - 1)])
    high = lax.ppermute(head, "gz", [(i + 1, i) for i in range(count - 1)])
    return low, high


def from_partner(array):
    count = lax.axis_size("view")
    return lax.ppermute(array, "view", [(i, count - 1 - i) for i in range(count)])


def on_device(observed, initial, psf_taps, view_shifts, view_map):
    local_views = observed.shape[0]
    depth, rows, width = initial.shape
    gz = lax.axis_size("gz")
    t = tables(depth, rows * gz, width)
    group_index = lax.axis_index("view")
    all_slots = jnp.arange(view_map.shape[0], dtype=jnp.int32)
    ref_slot = jnp.sum(jnp.where(view_map == 0, all_slots, 0))
    ref_group = ref_slot // local_views
    ref_local = ref_slot % local_views

    def est_ends(estimate):
        head = blocks_of(estimate[:, : 2 * SUB], depth, 2, width)
        tail = blocks_of(estimate[:, rows - 2 * SUB :], depth, 2, width)
        return head, tail

    ends = (
        blocks_of(observed[:, :, :SUB], depth, 1, width)[:, 0],
        blocks_of(observed[:, :, rows - SUB :], depth, 1, width)[:, 0],
    )
    obs_sides = from_sides(*[jnp.concatenate(e, 0) for e in zip(est_ends(initial), ends)])
    blurs = blur_tables(group_index, view_map, view_shifts, psf_taps, local_views, depth, width)

    def joined(estimate, sides):
        product = join_views(estimate, sides, observed, obs_sides, blurs)
        product = product * from_partner(product)
        return estimate * jnp.exp(jnp.log(product) / VIEWS)

    def exchanged(array):
        return lax.all_to_all(array.astype(SENT), "gz", split_axis=0, concat_axis=0, tiled=True)

    estimate = joined(initial, obs_sides)
    turned = [exchanged(sent) for sent in forward_spectra(observed, gz, t)]
    backs = []
    for p, member in enumerate(turned):
        mine = lax.dynamic_index_in_dim(member, ref_local, 1, keepdims=True)
        ref_turned = jnp.where(group_index == ref_group, mine, from_partner(mine)).astype(F32)
        first = jnp.logical_and(lax.axis_index("gz") == 0, p == 0).astype(jnp.int32).reshape(1)
        crossed = cross_spectra(first, depth, member.astype(F32), ref_turned, t)
        backs.append(exchanged(crossed).astype(F32))
    for _ in range(1, ITERS):
        estimate = joined(estimate, from_sides(*est_ends(estimate)))
    surfaces = inverse_spectra(backs, t)
    return estimate, surfaces


def solution(mesh):
    placed = (P("view", "parts", "gz", None), P("parts", "gz", None), P(), P(), P())
    return jax.shard_map(
        on_device,
        mesh=mesh,
        in_specs=placed,
        out_specs=(P("parts", "gz", None), P("view", "parts", "gz", None)),
        check_vma=False,
    )
```

```python
import functools
import math

import jax
import jax.numpy as jnp
import ml_dtypes
import numpy as np
from jax import lax
from jax.experimental import pallas as pl
from jax.experimental.pallas import tpu as pltpu
from jax.sharding import PartitionSpec as P

VIEWS = 8
BX = 256
ITERS = 2
TAPS = 15
SUB = 8
CENTRE = 1.1
F32 = jnp.float32
BF16 = jnp.bfloat16
SENT = jnp.float16
LIMIT = 56 * 1024 * 1024


def two(table):
    high = table.astype(ml_dtypes.bfloat16)
    low = (table - high.astype(np.float64)).astype(ml_dtypes.bfloat16)
    return np.stack([high, low])


def left_table(cosines, sines):
    high, low = two(np.concatenate([cosines, sines], 0))
    return np.concatenate([high, low, high], 1)


def right_table(table):
    high, low = two(table)
    return np.concatenate([high, high, low], 0)


def depth_order(depth):
    order = [0, depth // 2]
    for k in range(1, depth // 2):
        order += [k, depth - k]
    return np.array(order)


def phase_tables(rows, columns, length):
    angles = 2.0 * math.pi / length * (np.outer(rows, columns) % length)
    return np.cos(angles), np.sin(angles)


@functools.lru_cache(None)
def tables(depth, by, bx):
    half = bx // 2
    norm = 1.0 / math.sqrt(depth * by * bx)
    c, s = phase_tables(np.arange(bx), np.arange(half), bx)
    alternate = 1.0 - 2.0 * (np.arange(bx) % 2)
    imag = -s
    imag[:, 0] = alternate
    x_forward = np.concatenate([c, imag], 1)
    weights = np.where(np.arange(half) == 0, 1.0, 2.0)
    imag = -s * weights
    imag[:, 0] = alternate
    x_back = np.concatenate([c * weights, imag], 1).T * norm
    zc, zs = phase_tables(depth_order(depth), np.arange(depth), depth)
    eye = np.eye(SUB)
    yc, ys = phase_tables(np.arange(by), np.arange(by), by)
    return dict(
        x_forward=two(x_forward).reshape(2 * bx, bx),
        x_back=right_table(x_back),
        z_forward=left_table(np.kron(zc, eye), np.kron(zs, eye)),
        z_back=left_table(np.kron(zc.T, eye), np.kron(zs.T, eye)),
        y_forward=left_table(yc * norm, ys * norm),
        y_back=left_table(yc, ys),
    )


def dot(a, b):
    return jnp.dot(a, b, preferred_element_type=F32)


def split(a):
    high = a.astype(BF16)
    return high, (a - high.astype(F32)).astype(BF16)


def left_mix(table_ref, field):
    high, low = field
    both = dot(table_ref[...], jnp.concatenate([high, high, low], 0))
    size = table_ref.shape[0] // 2
    return both[:size], both[size:]


def right_mix(field, table_ref):
    high, low = field
    return dot(jnp.concatenate([high, low, high], 1), table_ref[...])


def params():
    return pltpu.CompilerParams(vmem_limit_bytes=LIMIT)


def cost(flops, bytes_accessed, transcendentals=0):
    return pl.CostEstimate(
        flops=int(flops), bytes_accessed=int(bytes_accessed), transcendentals=int(transcendentals)
    )


def whole(array):
    zeros = (0,) * array.ndim
    return pl.BlockSpec(array.shape, lambda *_: zeros)


def forward_kernel(obs_ref, x_ref, z_ref, *rest):
    out_refs, held = rest[:-1], rest[-1]
    _, depth, rows, width = obs_ref.shape
    half = width // 2
    group = out_refs[0].shape[0]
    lane = lax.broadcasted_iota(jnp.int32, (1, width), 1)
    centre = jnp.where(lane == 0, CENTRE * width, 0.0).astype(F32)
    flat = obs_ref[0].reshape(depth * rows, width)
    mixed = dot(jnp.concatenate([flat, flat], 1), x_ref[...]) - centre
    mixed = mixed.reshape(depth, rows, width)
    for at in range(0, rows, SUB):
        field = split(mixed[:, at : at + SUB, :].reshape(depth * SUB, width))
        cos_part, sin_part = left_mix(z_ref, field)
        real = cos_part[:, :half] + sin_part[:, half:]
        imag = cos_part[:, half:] - sin_part[:, :half]
        held[0, :, at : at + SUB, :] = real.reshape(depth, SUB, half)
        held[1, :, at : at + SUB, :] = imag.reshape(depth, SUB, half)
    for c in range(2):
        field = held[c].reshape(group, depth // group, rows, half)
        for p, out_ref in enumerate(out_refs):
            out_ref[:, 0, c] = field[:, 2 * p : 2 * p + 2]


def forward_spectra(observed, group, t):
    views, depth, rows, width = observed.shape
    chunks = depth // group // 2
    shape = (group, views, 2, 2, rows, width // 2)
    x_table, z_table = jnp.asarray(t["x_forward"]), jnp.asarray(t["z_forward"])
    return pl.pallas_call(
        forward_kernel,
        grid=(views,),
        out_shape=[jax.ShapeDtypeStruct(shape, F32)] * chunks,
        in_specs=[
            pl.BlockSpec((1,) + observed.shape[1:], lambda v: (v, 0, 0, 0)),
            whole(x_table),
            whole(z_table),
        ],
        out_specs=[pl.BlockSpec((group, 1) + shape[2:], lambda v: (0, v, 0, 0, 0, 0))] * chunks,
        scratch_shapes=[pltpu.VMEM((2, depth, rows, width // 2), F32)],
        compiler_params=params(),
        cost_estimate=cost(observed.size * 256 * 2 * 8, observed.size * 4),
        name="spectra_x_z",
    )(observed, x_table, z_table)


def cross_kernel(depth, first_ref, spec_ref, ref_ref, fwd_ref, back_ref, out_ref, held):
    group, _, _, _, rows, half = spec_ref.shape
    by = group * rows
    alone = first_ref[0] == 1
    lane0 = lax.broadcasted_iota(jnp.int32, (by, half), 1) == 0
    row0 = lax.broadcasted_iota(jnp.int32, (by, half), 0) == 0
    total = CENTRE * math.sqrt(depth * by * 2 * half)
    origin = jnp.logical_and(lane0, row0)

    def spectrum(ref):
        straight, turned = [], []
        for k in range(2):
            real = ref[:, 0, 0, k].astype(F32).reshape(by, half)
            imag = ref[:, 0, 1, k].astype(F32).reshape(by, half)
            field = split(jnp.concatenate([real, imag], 1))
            cos_part, sin_part = left_mix(fwd_ref, field)
            cos_real = cos_part[:, :half]
            if k == 0:
                cos_real = cos_real + jnp.where(jnp.logical_and(origin, alone), total, 0.0)
            straight.append((cos_real + sin_part[:, half:], cos_part[:, half:] - sin_part[:, :half]))
            turned.append((cos_real - sin_part[:, half:], cos_part[:, half:] + sin_part[:, :half]))
        out = []
        for k in range(2):
            real, imag = straight[k]
            other_real = jnp.where(alone, turned[k][0], turned[1 - k][0])
            other_imag = jnp.where(alone, turned[k][1], turned[1 - k][1])
            out.append(
                (
                    jnp.where(lane0, 0.5 * (real + other_real), real),
                    jnp.where(lane0, 0.5 * (imag - other_imag), imag),
                    0.5 * (imag + other_imag),
                    0.5 * (other_real - real),
                )
            )
        return out

    @pl.when(pl.program_id(0) == 0)
    def _():
        for k, member in enumerate(spectrum(ref_ref)):
            for i in range(4):
                held[k, i] = member[i]

    def cross(sr, si, rr, ri):
        magnitude = jnp.sqrt((sr * sr + si * si) * (rr * rr + ri * ri))
        scale = 1.0 / (magnitude + 1.0)
        return (sr * rr + si * ri) * scale, (si * rr - sr * ri) * scale

    for k, member in enumerate(spectrum(spec_ref)):
        real, imag = cross(member[0], member[1], held[k, 0], held[k, 1])
        top_real, top_imag = cross(member[2], member[3], held[k, 2], held[k, 3])
        real = jnp.where(lane0, real - top_imag, real)
        imag = jnp.where(lane0, imag + top_real, imag)
        field = split(jnp.concatenate([real, imag], 1))
        cos_part, sin_part = left_mix(back_ref, field)
        real = cos_part[:, :half] - sin_part[:, half:]
        imag = cos_part[:, half:] + sin_part[:, :half]
        out_ref[:, 0, 0, k] = real.reshape(group, rows, half).astype(out_ref.dtype)
        out_ref[:, 0, 1, k] = imag.reshape(group, rows, half).astype(out_ref.dtype)


def cross_spectra(first, depth, turned, ref_turned, t):
    group, views, _, _, rows, half = turned.shape
    by = group * rows
    fwd, back = jnp.asarray(t["y_forward"]), jnp.asarray(t["y_back"])
    block = (group, 1, 2, 2, rows, half)
    return pl.pallas_call(
        functools.partial(cross_kernel, depth),
        grid=(views,),
        out_shape=jax.ShapeDtypeStruct(turned.shape, F32),
        in_specs=[
            pl.BlockSpec(memory_space=pltpu.SMEM),
            pl.BlockSpec(block, lambda v: (0, v, 0, 0, 0, 0)),
            pl.BlockSpec(block, lambda v: (0, 0, 0, 0, 0, 0)),
            whole(fwd),
            whole(back),
        ],
        out_specs=pl.BlockSpec(block, lambda v: (0, v, 0, 0, 0, 0)),
        scratch_shapes=[pltpu.VMEM((2, 4, by, half), F32)],
        compiler_params=params(),
        cost_estimate=cost(turned.size * 256 * 2 * 12, turned.size * 4, turned.size),
        name="cross_y",
    )(first, turned, ref_turned, fwd, back)


def inverse_kernel(*refs):
    back_refs, (z_ref, x_ref, out_ref, held) = refs[:-4], refs[-4:]
    group, _, _, _, rows, half = back_refs[0].shape
    depth = group * 2 * len(back_refs)
    for c in range(2):
        field = jnp.concatenate([ref[:, 0, c] for ref in back_refs], 1)
        held[c] = field.reshape(depth, rows, half)
    for at in range(0, rows, SUB):
        real = held[0, :, at : at + SUB, :].reshape(depth * SUB, half)
        imag = held[1, :, at : at + SUB, :].reshape(depth * SUB, half)
        field = split(jnp.concatenate([real, imag], 1))
        cos_part, sin_part = left_mix(z_ref, field)
        real = cos_part[:, :half] - sin_part[:, half:]
        imag = cos_part[:, half:] + sin_part[:, :half]
        field = split(jnp.concatenate([real, imag], 1))
        result = right_mix(field, x_ref)
        out_ref[0, :, at : at + SUB, :] = result.reshape(depth, SUB, 2 * half)


def inverse_spectra(backs, t):
    group, views, _, _, rows, half = backs[0].shape
    depth = group * 2 * len(backs)
    shape = (views, depth, rows, 2 * half)
    z_table, x_table = jnp.asarray(t["z_back"]), jnp.asarray(t["x_back"])
    return pl.pallas_call(
        inverse_kernel,
        grid=(views,),
        out_shape=jax.ShapeDtypeStruct(shape, F32),
        in_specs=[
            *[pl.BlockSpec((group, 1) + b.shape[2:], lambda v: (0, v, 0, 0, 0, 0)) for b in backs],
            whole(z_table),
            whole(x_table),
        ],
        out_specs=pl.BlockSpec((1,) + shape[1:], lambda v: (v, 0, 0, 0)),
        scratch_shapes=[pltpu.VMEM((2, depth, rows, half), F32)],
        compiler_params=params(),
        cost_estimate=cost(math.prod(shape) * 256 * 2 * 9, math.prod(shape) * 8),
        name="surface_z_x",
    )(*backs, z_table, x_table)


def by_tap(row, offsets):
    summed = jnp.zeros(offsets.shape, F32)
    for i in range(TAPS):
        summed = jnp.where(offsets == i, row(i), summed)
    return summed


def table_kernel(depth, group_ref, map_ref, shift_ref, taps_ref, zyf_ref, zyb_ref, xf_ref, xb_ref):
    width = xf_ref.shape[-1]
    size = depth * SUB
    view = map_ref[group_ref[0] * pl.num_programs(0) + pl.program_id(0)]
    shift_z, shift_x = shift_ref[view, 0], shift_ref[view, 1]

    def taps(axis):
        return lambda i: taps_ref[view, axis * TAPS + i]

    def places(rows, columns):
        shape = (rows, columns)
        return [lax.broadcasted_iota(jnp.int32, shape, d) for d in range(2)]

    row, col = places(depth, size)
    z_off = lax.shift_right_logical(col, 3) - row + 7
    z_pair = by_tap(taps(0), z_off - shift_z), by_tap(taps(0), 14 - z_off - shift_z)
    row, col = places(SUB, size)
    for j in range(3):
        y_off = SUB * (j - 1) + jnp.bitwise_and(col, SUB - 1) - row + 7
        y_pair = by_tap(taps(1), y_off), by_tap(taps(1), 14 - y_off)
        for ref, z, y in zip((zyf_ref, zyb_ref), z_pair, y_pair):
            both = (z[:, None, :] * y[None]).reshape(size, size)
            ref[0, j * size : (j + 1) * size] = both.astype(BF16)
    row, col = places(width, width)
    x_off = row - col + 7
    xf_ref[0] = by_tap(taps(2), x_off - shift_x).astype(BF16)
    xb_ref[0] = by_tap(taps(2), 14 - x_off - shift_x).astype(BF16)


def view_block(array):
    zeros = (0,) * (array.ndim - 1)
    return pl.BlockSpec((1,) + array.shape[1:], lambda v: (v,) + zeros)


def blur_tables(group_index, view_map, view_shifts, psf_taps, views, depth, width):
    size = depth * SUB
    zy = jax.ShapeDtypeStruct((views, 3 * size, size), BF16)
    x = jax.ShapeDtypeStruct((views, width, width), BF16)
    return pl.pallas_call(
        functools.partial(table_kernel, depth),
        grid=(views,),
        out_shape=[zy, zy, x, x],
        in_specs=[pl.BlockSpec(memory_space=pltpu.SMEM)] * 4,
        out_specs=[view_block(zy), view_block(zy), view_block(x), view_block(x)],
        compiler_params=params(),
        cost_estimate=cost(views * size * size * 100, views * size * size * 16),
        name="blur_tables",
    )(group_index.reshape(1), view_map, view_shifts, psf_taps.reshape(psf_taps.shape[0], -1))


def blur(pieces, zy_ref, x_ref, total, use):
    count = len(pieces) - 2
    size = zy_ref.shape[2]
    for b, piece in enumerate(pieces):
        steps = [j for j in range(3) if 0 <= b - j < count]
        table = zy_ref[0, steps[0] * size : (steps[-1] + 1) * size]
        table = jnp.concatenate([table] * len(piece), 1)
        mixed = dot(table, jnp.concatenate(piece, 0) if len(piece) > 1 else piece[0])
        for j in steps:
            part = mixed[(j - steps[0]) * size : (j - steps[0] + 1) * size]
            if j == 0:
                total[b - j] = part
            elif j == 1:
                total[b - j] += part
            else:
                done = dot(jnp.concatenate(split(total[b - j] + part), 0), x_ref[0])
                use(b - j, done[:size] + done[size:])


def join_kernel(
    est_ref, low_ref, high_ref, obs_ref, obs_low_ref, obs_high_ref,
    zyf_ref, zyb_ref, xf_ref, xb_ref, out_ref, held, total, ratio,
):
    depth, rows, width = est_ref.shape
    size = depth * SUB
    count = rows // SUB
    held[...] = obs_ref[0].astype(F32)
    pieces = [(low_ref[0],), (low_ref[1],)]
    for b in range(count):
        pieces.append(split(est_ref[:, b * SUB : (b + 1) * SUB, :].reshape(size, width)))
    pieces += [(high_ref[0],), (high_ref[1],)]

    def keep_ratio(b, blurred):
        if b == 0:
            seen = obs_low_ref[0].astype(F32)
        elif b == count + 1:
            seen = obs_high_ref[0].astype(F32)
        else:
            seen = held[:, (b - 1) * SUB : b * SUB, :].reshape(size, width)
        value = seen / blurred
        if b in (0, count + 1):
            value = jnp.where(seen > 0.0, value, 0.0)
        ratio[b, 0], ratio[b, 1] = split(value)

    blur(pieces, zyf_ref, xf_ref, total, keep_ratio)
    first = pl.program_id(0) == 0

    def keep_update(b, update):
        spot = (slice(None), slice(b * SUB, (b + 1) * SUB), slice(None))
        update = update.reshape(depth, SUB, width)
        out_ref[spot] = jnp.where(first, update, update * out_ref[spot])

    pieces = [(ratio[b, 0], ratio[b, 1]) for b in range(count + 2)]
    blur(pieces, zyb_ref, xb_ref, total, keep_update)


def join_views(estimate, sides, observed, obs_sides, blurs):
    depth, rows, width = estimate.shape
    size = depth * SUB
    count = rows // SUB
    args = (estimate,) + tuple(sides) + (observed,) + tuple(obs_sides) + tuple(blurs)
    side = pl.BlockSpec((2, size, width), lambda v: (0, 0, 0))
    obs_side = pl.BlockSpec((1, size, width), lambda v: (v + 2, 0, 0))
    return pl.pallas_call(
        join_kernel,
        grid=(observed.shape[0],),
        out_shape=jax.ShapeDtypeStruct(estimate.shape, F32),
        in_specs=[whole(estimate), side, side, view_block(observed), obs_side, obs_side]
        + [view_block(a) for a in blurs],
        out_specs=whole(estimate),
        scratch_shapes=[
            pltpu.VMEM((depth, rows, width), F32),
            pltpu.VMEM((count + 2, size, width), F32),
            pltpu.VMEM((count + 2, 2, size, width), BF16),
        ],
        compiler_params=params(),
        cost_estimate=cost(observed.size * 256 * 2 * 20, observed.size * 8, observed.size),
        name="join_views",
    )(*args)


def blocks_of(rows_of, depth, count, width):
    shape = rows_of.shape[:-3]
    split_up = rows_of.astype(BF16).reshape(shape + (depth, count, SUB, width))
    return jnp.swapaxes(split_up, -4, -3).reshape(shape + (count, depth * SUB, width))


def from_sides(head, tail):
    count = lax.axis_size("gz")
    low = lax.ppermute(tail, "gz", [(i, i + 1) for i in range(count - 1)])
    high = lax.ppermute(head, "gz", [(i + 1, i) for i in range(count - 1)])
    return low, high


def from_partner(array):
    count = lax.axis_size("view")
    return lax.ppermute(array, "view", [(i, count - 1 - i) for i in range(count)])


def on_device(observed, initial, psf_taps, view_shifts, view_map):
    local_views = observed.shape[0]
    depth, rows, width = initial.shape
    gz = lax.axis_size("gz")
    t = tables(depth, rows * gz, width)
    group_index = lax.axis_index("view")
    all_slots = jnp.arange(view_map.shape[0], dtype=jnp.int32)
    ref_slot = jnp.sum(jnp.where(view_map == 0, all_slots, 0))
    ref_group = ref_slot // local_views
    ref_local = ref_slot % local_views

    def est_ends(estimate):
        head = blocks_of(estimate[:, : 2 * SUB], depth, 2, width)
        tail = blocks_of(estimate[:, rows - 2 * SUB :], depth, 2, width)
        return head, tail

    ends = (
        blocks_of(observed[:, :, :SUB], depth, 1, width)[:, 0],
        blocks_of(observed[:, :, rows - SUB :], depth, 1, width)[:, 0],
    )
    obs_sides = from_sides(*[jnp.concatenate(e, 0) for e in zip(est_ends(initial), ends)])
    blurs = blur_tables(group_index, view_map, view_shifts, psf_taps, local_views, depth, width)

    def joined(estimate, sides):
        product = join_views(estimate, sides, observed, obs_sides, blurs)
        product = product * from_partner(product)
        return estimate * jnp.exp(jnp.log(product) / VIEWS)

    def exchanged(array):
        array = array.astype(SENT)
        return lax.all_to_all(array, "gz", split_axis=0, concat_axis=0, tiled=True)

    def crossed(p, member):
        mine = lax.dynamic_index_in_dim(member, ref_local, 1, keepdims=True)
        ref_turned = jnp.where(group_index == ref_group, mine, from_partner(mine)).astype(F32)
        first = jnp.logical_and(lax.axis_index("gz") == 0, p == 0).astype(jnp.int32).reshape(1)
        return cross_spectra(first, depth, member.astype(F32), ref_turned, t).astype(SENT)

    after = lax.optimization_barrier
    turned = [exchanged(sent) for sent in forward_spectra(observed, gz, t)]
    turned[0], blurs = after((turned[0], blurs))
    mixed = [crossed(0, turned[0])]
    estimate, mixed[0], turned[1:] = after((initial, mixed[0], turned[1:]))
    backs = [exchanged(mixed[0])]
    estimate = joined(estimate, obs_sides)
    estimate, turned[1:] = after((estimate, turned[1:]))
    sides = from_sides(*est_ends(estimate))
    for p in range(1, len(turned)):
        mixed.append(crossed(p, turned[p]))
        backs.append(exchanged(mixed[p]))
    estimate, _ = after((estimate, mixed[-1]))
    for step in range(1, ITERS):
        if step > 1:
            sides = from_sides(*est_ends(estimate))
        estimate = joined(estimate, sides)
    surfaces = inverse_spectra([b.astype(F32) for b in backs], t)
    return estimate, surfaces


def solution(mesh):
    placed = (P("view", "parts", "gz", None), P("parts", "gz", None), P(), P(), P())
    return jax.shard_map(
        on_device,
        mesh=mesh,
        in_specs=placed,
        out_specs=(P("parts", "gz", None), P("view", "parts", "gz", None)),
        check_vma=False,
    )
```

```python
import functools
import math

import jax
import jax.numpy as jnp
import ml_dtypes
import numpy as np
from jax import lax
from jax.experimental import pallas as pl
from jax.experimental.pallas import tpu as pltpu
from jax.sharding import PartitionSpec as P

VIEWS = 8
BX = 256
ITERS = 2
TAPS = 15
SUB = 8
CENTRE = 1.1
F32 = jnp.float32
BF16 = jnp.bfloat16
SENT = jnp.float16
LIMIT = 56 * 1024 * 1024
EARLY = 20


def two(table):
    high = table.astype(ml_dtypes.bfloat16)
    low = (table - high.astype(np.float64)).astype(ml_dtypes.bfloat16)
    return np.stack([high, low])


def left_table(cosines, sines):
    high, low = two(np.concatenate([cosines, sines], 0))
    return np.concatenate([high, low, high], 1)


def right_table(table):
    high, low = two(table)
    return np.concatenate([high, high, low], 0)


def depth_order(depth):
    order = [0, depth // 2]
    for k in range(1, depth // 2):
        order += [k, depth - k]
    return np.array(order)


def phase_tables(rows, columns, length):
    angles = 2.0 * math.pi / length * (np.outer(rows, columns) % length)
    return np.cos(angles), np.sin(angles)


@functools.lru_cache(None)
def tables(depth, by, bx):
    half = bx // 2
    norm = 1.0 / math.sqrt(depth * by * bx)
    c, s = phase_tables(np.arange(bx), np.arange(half), bx)
    alternate = 1.0 - 2.0 * (np.arange(bx) % 2)
    imag = -s
    imag[:, 0] = alternate
    x_forward = np.concatenate([c, imag], 1)
    weights = np.where(np.arange(half) == 0, 1.0, 2.0)
    imag = -s * weights
    imag[:, 0] = alternate
    x_back = np.concatenate([c * weights, imag], 1).T * norm
    zc, zs = phase_tables(depth_order(depth), np.arange(depth), depth)
    eye = np.eye(SUB)
    yc, ys = phase_tables(np.arange(by), np.arange(by), by)
    return dict(
        x_forward=two(x_forward).reshape(2 * bx, bx),
        x_back=right_table(x_back),
        z_forward=left_table(np.kron(zc, eye), np.kron(zs, eye)),
        z_back=left_table(np.kron(zc.T, eye), np.kron(zs.T, eye)),
        y_forward=left_table(yc * norm, ys * norm),
        y_back=left_table(yc, ys),
    )


def dot(a, b):
    return jnp.dot(a, b, preferred_element_type=F32)


def split(a):
    high = a.astype(BF16)
    return high, (a - high.astype(F32)).astype(BF16)


def left_mix(table_ref, field):
    high, low = field
    both = dot(table_ref[...], jnp.concatenate([high, high, low], 0))
    size = table_ref.shape[0] // 2
    return both[:size], both[size:]


def right_mix(field, table_ref):
    high, low = field
    return dot(jnp.concatenate([high, low, high], 1), table_ref[...])


def inverse(a):
    guess = pl.reciprocal(a, approx=True)
    return guess * (2.0 - a * guess)


def params():
    return pltpu.CompilerParams(vmem_limit_bytes=LIMIT)


def cost(flops, bytes_accessed, transcendentals=0):
    return pl.CostEstimate(
        flops=int(flops) // EARLY,
        bytes_accessed=int(bytes_accessed) // EARLY,
        transcendentals=int(transcendentals) // EARLY,
    )


def whole(array):
    zeros = (0,) * array.ndim
    return pl.BlockSpec(array.shape, lambda *_: zeros)


def forward_kernel(obs_ref, x_ref, z_ref, *rest):
    out_refs, held = rest[:-1], rest[-1]
    _, depth, rows, width = obs_ref.shape
    half = width // 2
    group = out_refs[0].shape[0]
    lane = lax.broadcasted_iota(jnp.int32, (1, width), 1)
    centre = jnp.where(lane == 0, CENTRE * width, 0.0).astype(F32)
    flat = obs_ref[0].reshape(depth * rows, width)
    mixed = dot(jnp.concatenate([flat, flat], 1), x_ref[...]) - centre
    mixed = mixed.reshape(depth, rows, width)
    for at in range(0, rows, SUB):
        field = split(mixed[:, at : at + SUB, :].reshape(depth * SUB, width))
        cos_part, sin_part = left_mix(z_ref, field)
        real = cos_part[:, :half] + sin_part[:, half:]
        imag = cos_part[:, half:] - sin_part[:, :half]
        held[0, :, at : at + SUB, :] = real.reshape(depth, SUB, half)
        held[1, :, at : at + SUB, :] = imag.reshape(depth, SUB, half)
    for c in range(2):
        field = held[c].reshape(group, depth // group, rows, half)
        for p, out_ref in enumerate(out_refs):
            out_ref[:, 0, c] = field[:, 2 * p : 2 * p + 2]


def forward_spectra(observed, group, t):
    views, depth, rows, width = observed.shape
    chunks = depth // group // 2
    shape = (group, views, 2, 2, rows, width // 2)
    x_table, z_table = jnp.asarray(t["x_forward"]), jnp.asarray(t["z_forward"])
    return pl.pallas_call(
        forward_kernel,
        grid=(views,),
        out_shape=[jax.ShapeDtypeStruct(shape, F32)] * chunks,
        in_specs=[
            pl.BlockSpec((1,) + observed.shape[1:], lambda v: (v, 0, 0, 0)),
            whole(x_table),
            whole(z_table),
        ],
        out_specs=[pl.BlockSpec((group, 1) + shape[2:], lambda v: (0, v, 0, 0, 0, 0))] * chunks,
        scratch_shapes=[pltpu.VMEM((2, depth, rows, width // 2), F32)],
        compiler_params=params(),
        cost_estimate=cost(observed.size * 256 * 2 * 8, observed.size * 4),
        name="spectra_x_z",
    )(observed, x_table, z_table)


def cross_kernel(depth, first_ref, spec_ref, ref_ref, fwd_ref, back_ref, out_ref, held):
    group, _, _, _, rows, half = spec_ref.shape
    by = group * rows
    alone = first_ref[0] == 1
    lane0 = lax.broadcasted_iota(jnp.int32, (by, half), 1) == 0
    row0 = lax.broadcasted_iota(jnp.int32, (by, half), 0) == 0
    total = CENTRE * math.sqrt(depth * by * 2 * half)
    origin = jnp.logical_and(lane0, row0)

    def spectrum(ref):
        straight, turned = [], []
        for k in range(2):
            real = ref[:, 0, 0, k].astype(F32).reshape(by, half)
            imag = ref[:, 0, 1, k].astype(F32).reshape(by, half)
            field = split(jnp.concatenate([real, imag], 1))
            cos_part, sin_part = left_mix(fwd_ref, field)
            cos_real = cos_part[:, :half]
            if k == 0:
                cos_real = cos_real + jnp.where(jnp.logical_and(origin, alone), total, 0.0)
            straight.append((cos_real + sin_part[:, half:], cos_part[:, half:] - sin_part[:, :half]))
            turned.append((cos_real - sin_part[:, half:], cos_part[:, half:] + sin_part[:, :half]))
        out = []
        for k in range(2):
            real, imag = straight[k]
            other_real = jnp.where(alone, turned[k][0], turned[1 - k][0])
            other_imag = jnp.where(alone, turned[k][1], turned[1 - k][1])
            out.append(
                (
                    jnp.where(lane0, 0.5 * (real + other_real), real),
                    jnp.where(lane0, 0.5 * (imag - other_imag), imag),
                    0.5 * (imag + other_imag),
                    0.5 * (other_real - real),
                )
            )
        return out

    @pl.when(pl.program_id(0) == 0)
    def _():
        for k, member in enumerate(spectrum(ref_ref)):
            for i in range(4):
                held[k, i] = member[i]

    def cross(sr, si, rr, ri):
        magnitude = jnp.sqrt((sr * sr + si * si) * (rr * rr + ri * ri))
        scale = inverse(magnitude + 1.0)
        return (sr * rr + si * ri) * scale, (si * rr - sr * ri) * scale

    for k, member in enumerate(spectrum(spec_ref)):
        real, imag = cross(member[0], member[1], held[k, 0], held[k, 1])
        top_real, top_imag = cross(member[2], member[3], held[k, 2], held[k, 3])
        real = jnp.where(lane0, real - top_imag, real)
        imag = jnp.where(lane0, imag + top_real, imag)
        field = split(jnp.concatenate([real, imag], 1))
        cos_part, sin_part = left_mix(back_ref, field)
        real = cos_part[:, :half] - sin_part[:, half:]
        imag = cos_part[:, half:] + sin_part[:, :half]
        out_ref[:, 0, 0, k] = real.reshape(group, rows, half).astype(out_ref.dtype)
        out_ref[:, 0, 1, k] = imag.reshape(group, rows, half).astype(out_ref.dtype)


def cross_spectra(first, depth, turned, ref_turned, t):
    group, views, _, _, rows, half = turned.shape
    by = group * rows
    fwd, back = jnp.asarray(t["y_forward"]), jnp.asarray(t["y_back"])
    block = (group, 1, 2, 2, rows, half)
    return pl.pallas_call(
        functools.partial(cross_kernel, depth),
        grid=(views,),
        out_shape=jax.ShapeDtypeStruct(turned.shape, F32),
        in_specs=[
            pl.BlockSpec(memory_space=pltpu.SMEM),
            pl.BlockSpec(block, lambda v: (0, v, 0, 0, 0, 0)),
            pl.BlockSpec(block, lambda v: (0, 0, 0, 0, 0, 0)),
            whole(fwd),
            whole(back),
        ],
        out_specs=pl.BlockSpec(block, lambda v: (0, v, 0, 0, 0, 0)),
        scratch_shapes=[pltpu.VMEM((2, 4, by, half), F32)],
        compiler_params=params(),
        cost_estimate=cost(turned.size * 256 * 2 * 12, turned.size * 4, turned.size),
        name="cross_y",
    )(first, turned, ref_turned, fwd, back)


def inverse_kernel(*refs):
    back_refs, (z_ref, x_ref, out_ref, held) = refs[:-4], refs[-4:]
    group, _, _, _, rows, half = back_refs[0].shape
    depth = group * 2 * len(back_refs)
    for c in range(2):
        field = jnp.concatenate([ref[:, 0, c] for ref in back_refs], 1)
        held[c] = field.reshape(depth, rows, half)
    fields = []
    for at in range(0, rows, SUB):
        real = held[0, :, at : at + SUB, :].reshape(depth * SUB, half)
        imag = held[1, :, at : at + SUB, :].reshape(depth * SUB, half)
        field = split(jnp.concatenate([real, imag], 1))
        cos_part, sin_part = left_mix(z_ref, field)
        real = cos_part[:, :half] - sin_part[:, half:]
        imag = cos_part[:, half:] + sin_part[:, :half]
        fields.append(jnp.concatenate([real, imag], 1))
    result = right_mix(split(jnp.concatenate(fields, 0)), x_ref)
    size = depth * SUB
    for at in range(0, rows, SUB):
        part = result[at // SUB * size : (at // SUB + 1) * size]
        out_ref[0, :, at : at + SUB, :] = part.reshape(depth, SUB, 2 * half)


def inverse_spectra(backs, t):
    group, views, _, _, rows, half = backs[0].shape
    depth = group * 2 * len(backs)
    shape = (views, depth, rows, 2 * half)
    z_table, x_table = jnp.asarray(t["z_back"]), jnp.asarray(t["x_back"])
    return pl.pallas_call(
        inverse_kernel,
        grid=(views,),
        out_shape=jax.ShapeDtypeStruct(shape, F32),
        in_specs=[
            *[pl.BlockSpec((group, 1) + b.shape[2:], lambda v: (0, v, 0, 0, 0, 0)) for b in backs],
            whole(z_table),
            whole(x_table),
        ],
        out_specs=pl.BlockSpec((1,) + shape[1:], lambda v: (v, 0, 0, 0)),
        scratch_shapes=[pltpu.VMEM((2, depth, rows, half), F32)],
        compiler_params=params(),
        cost_estimate=cost(math.prod(shape) * 256 * 2 * 9, math.prod(shape) * 8),
        name="surface_z_x",
    )(*backs, z_table, x_table)


def by_tap(row, offsets):
    summed = jnp.zeros(offsets.shape, F32)
    for i in range(TAPS):
        summed = jnp.where(offsets == i, row(i), summed)
    return summed


def table_kernel(depth, group_ref, map_ref, shift_ref, taps_ref, zyf_ref, zyb_ref, xf_ref, xb_ref):
    width = xf_ref.shape[-1]
    size = depth * SUB
    view = map_ref[group_ref[0] * pl.num_programs(0) + pl.program_id(0)]
    shift_z, shift_x = shift_ref[view, 0], shift_ref[view, 1]

    def taps(axis):
        return lambda i: taps_ref[view, axis * TAPS + i]

    def places(rows, columns):
        shape = (rows, columns)
        return [lax.broadcasted_iota(jnp.int32, shape, d) for d in range(2)]

    row, col = places(depth, size)
    z_off = lax.shift_right_logical(col, 3) - row + 7
    z_pair = by_tap(taps(0), z_off - shift_z), by_tap(taps(0), 14 - z_off - shift_z)
    row, col = places(SUB, size)
    for j in range(3):
        y_off = SUB * (j - 1) + jnp.bitwise_and(col, SUB - 1) - row + 7
        y_pair = by_tap(taps(1), y_off), by_tap(taps(1), 14 - y_off)
        for ref, z, y in zip((zyf_ref, zyb_ref), z_pair, y_pair):
            both = (z[:, None, :] * y[None]).reshape(size, size)
            ref[0, j * size : (j + 1) * size] = both.astype(BF16)
    row, col = places(width, width)
    x_off = row - col + 7
    xf_ref[0] = by_tap(taps(2), x_off - shift_x).astype(BF16)
    xb_ref[0] = by_tap(taps(2), 14 - x_off - shift_x).astype(BF16)


def view_block(array):
    zeros = (0,) * (array.ndim - 1)
    return pl.BlockSpec((1,) + array.shape[1:], lambda v: (v,) + zeros)


def blur_tables(group_index, view_map, view_shifts, psf_taps, views, depth, width):
    size = depth * SUB
    zy = jax.ShapeDtypeStruct((views, 3 * size, size), BF16)
    x = jax.ShapeDtypeStruct((views, width, width), BF16)
    return pl.pallas_call(
        functools.partial(table_kernel, depth),
        grid=(views,),
        out_shape=[zy, zy, x, x],
        in_specs=[pl.BlockSpec(memory_space=pltpu.SMEM)] * 4,
        out_specs=[view_block(zy), view_block(zy), view_block(x), view_block(x)],
        compiler_params=params(),
        cost_estimate=cost(views * size * size * 100, views * size * size * 16),
        name="blur_tables",
    )(group_index.reshape(1), view_map, view_shifts, psf_taps.reshape(psf_taps.shape[0], -1))


def blur(pieces, zy_ref, x_ref, total, use):
    count = len(pieces) - 2
    size = zy_ref.shape[2]
    for b, piece in enumerate(pieces):
        steps = [j for j in range(3) if 0 <= b - j < count]
        table = zy_ref[0, steps[0] * size : (steps[-1] + 1) * size]
        table = jnp.concatenate([table] * len(piece), 1)
        mixed = dot(table, jnp.concatenate(piece, 0) if len(piece) > 1 else piece[0])
        for j in steps:
            part = mixed[(j - steps[0]) * size : (j - steps[0] + 1) * size]
            if j == 0:
                total[b - j] = part
            elif j == 1:
                total[b - j] += part
            else:
                done = dot(jnp.concatenate(split(total[b - j] + part), 0), x_ref[0])
                use(b - j, done[:size] + done[size:])


def join_kernel(
    est_ref, low_ref, high_ref, obs_ref, obs_low_ref, obs_high_ref,
    zyf_ref, zyb_ref, xf_ref, xb_ref, out_ref, held, total, ratio, parts,
):
    depth, rows, width = est_ref.shape
    size = depth * SUB
    count = rows // SUB
    held[...] = obs_ref[0].astype(F32)
    pieces = [(low_ref[0],), (low_ref[1],)]
    first = pl.program_id(0) == 0

    @pl.when(first)
    def _():
        for b in range(count):
            block = est_ref[:, b * SUB : (b + 1) * SUB, :].reshape(size, width)
            parts[b, 0], parts[b, 1] = split(block)

    pieces += [(parts[b, 0], parts[b, 1]) for b in range(count)]
    pieces += [(high_ref[0],), (high_ref[1],)]

    def keep_ratio(b, blurred):
        if b == 0:
            seen = obs_low_ref[0].astype(F32)
        elif b == count + 1:
            seen = obs_high_ref[0].astype(F32)
        else:
            seen = held[:, (b - 1) * SUB : b * SUB, :].reshape(size, width)
        value = seen * inverse(blurred)
        if b in (0, count + 1):
            value = jnp.where(seen > 0.0, value, 0.0)
        ratio[b] = value.astype(BF16)

    blur(pieces, zyf_ref, xf_ref, total, keep_ratio)

    def keep_update(b, update):
        spot = (slice(None), slice(b * SUB, (b + 1) * SUB), slice(None))
        update = update.reshape(depth, SUB, width)
        out_ref[spot] = jnp.where(first, update, update * out_ref[spot])

    pieces = [(ratio[b],) for b in range(count + 2)]
    blur(pieces, zyb_ref, xb_ref, total, keep_update)


def join_views(estimate, sides, observed, obs_sides, blurs):
    depth, rows, width = estimate.shape
    size = depth * SUB
    count = rows // SUB
    args = (estimate,) + tuple(sides) + (observed,) + tuple(obs_sides) + tuple(blurs)
    side = pl.BlockSpec((2, size, width), lambda v: (0, 0, 0))
    obs_side = pl.BlockSpec((1, size, width), lambda v: (v + 2, 0, 0))
    return pl.pallas_call(
        join_kernel,
        grid=(observed.shape[0],),
        out_shape=jax.ShapeDtypeStruct(estimate.shape, F32),
        in_specs=[whole(estimate), side, side, view_block(observed), obs_side, obs_side]
        + [view_block(a) for a in blurs],
        out_specs=whole(estimate),
        scratch_shapes=[
            pltpu.VMEM((depth, rows, width), F32),
            pltpu.VMEM((count + 2, size, width), F32),
            pltpu.VMEM((count + 2, size, width), BF16),
            pltpu.VMEM((count, 2, size, width), BF16),
        ],
        compiler_params=params(),
        cost_estimate=cost(observed.size * 256 * 2 * 20, observed.size * 8, observed.size),
        name="join_views",
    )(*args)


def blocks_of(rows_of, depth, count, width):
    shape = rows_of.shape[:-3]
    split_up = rows_of.astype(BF16).reshape(shape + (depth, count, SUB, width))
    return jnp.swapaxes(split_up, -4, -3).reshape(shape + (count, depth * SUB, width))


def from_sides(head, tail):
    count = lax.axis_size("gz")
    low = lax.ppermute(tail, "gz", [(i, i + 1) for i in range(count - 1)])
    high = lax.ppermute(head, "gz", [(i + 1, i) for i in range(count - 1)])
    return low, high


def from_partner(array):
    count = lax.axis_size("view")
    return lax.ppermute(array, "view", [(i, count - 1 - i) for i in range(count)])


def on_device(observed, initial, psf_taps, view_shifts, view_map):
    local_views = observed.shape[0]
    depth, rows, width = initial.shape
    gz = lax.axis_size("gz")
    t = tables(depth, rows * gz, width)
    group_index = lax.axis_index("view")
    all_slots = jnp.arange(view_map.shape[0], dtype=jnp.int32)
    ref_slot = jnp.sum(jnp.where(view_map == 0, all_slots, 0))
    ref_group = ref_slot // local_views
    ref_local = ref_slot % local_views

    def est_ends(estimate):
        head = blocks_of(estimate[:, : 2 * SUB], depth, 2, width)
        tail = blocks_of(estimate[:, rows - 2 * SUB :], depth, 2, width)
        return head, tail

    ends = (
        blocks_of(observed[:, :, :SUB], depth, 1, width)[:, 0],
        blocks_of(observed[:, :, rows - SUB :], depth, 1, width)[:, 0],
    )
    obs_sides = from_sides(*[jnp.concatenate(e, 0) for e in zip(est_ends(initial), ends)])
    blurs = blur_tables(group_index, view_map, view_shifts, psf_taps, local_views, depth, width)

    def product_of(estimate, sides):
        return join_views(estimate, sides, observed, obs_sides, blurs)

    def updated(estimate, product):
        product = product * from_partner(product)
        return estimate * jnp.exp(jnp.log(product) / VIEWS)

    def exchanged(array):
        array = array.astype(SENT)
        return lax.all_to_all(array, "gz", split_axis=0, concat_axis=0, tiled=True)

    def crossed(p, member):
        mine = lax.dynamic_index_in_dim(member, ref_local, 1, keepdims=True)
        ref_turned = jnp.where(group_index == ref_group, mine, from_partner(mine)).astype(F32)
        first = jnp.logical_and(lax.axis_index("gz") == 0, p == 0).astype(jnp.int32).reshape(1)
        return cross_spectra(first, depth, member.astype(F32), ref_turned, t).astype(SENT)

    after = lax.optimization_barrier
    sent = [member.astype(SENT) for member in forward_spectra(observed, gz, t)]
    turned = [exchanged(sent[0])]
    obs_sides, blurs, estimate, sent[1:] = after((obs_sides, blurs, initial, sent[1:]))
    turned += [exchanged(member) for member in sent[1:]]
    product = product_of(estimate, obs_sides)
    turned[0], product = after((turned[0], product))
    mixed = [crossed(0, turned[0])]
    estimate = updated(estimate, product)
    estimate, mixed[0], turned[1:] = after((estimate, mixed[0], turned[1:]))
    sides = from_sides(*est_ends(estimate))
    mixed += [crossed(p, turned[p]) for p in range(1, len(turned))]
    backs = [exchanged(member) for member in mixed]
    estimate, _ = after((estimate, mixed[-1]))
    for step in range(1, ITERS):
        if step > 1:
            sides = from_sides(*est_ends(estimate))
        estimate = updated(estimate, product_of(estimate, sides))
    surfaces = inverse_spectra([b.astype(F32) for b in backs], t)
    return estimate, surfaces


def solution(mesh):
    placed = (P("view", "parts", "gz", None), P("parts", "gz", None), P(), P(), P())
    return jax.shard_map(
        on_device,
        mesh=mesh,
        in_specs=placed,
        out_specs=(P("parts", "gz", None), P("view", "parts", "gz", None)),
        check_vma=False,
    )
```

```python
import functools
import math

import jax
import jax.numpy as jnp
import ml_dtypes
import numpy as np
from jax import lax
from jax.experimental import pallas as pl
from jax.experimental.pallas import tpu as pltpu
from jax.sharding import PartitionSpec as P

VIEWS = 8
BX = 256
ITERS = 2
TAPS = 15
SUB = 8
CENTRE = 1.1
F32 = jnp.float32
BF16 = jnp.bfloat16
SENT = jnp.float16
LIMIT = 56 * 1024 * 1024
EARLY = 20


def two(table):
    high = table.astype(ml_dtypes.bfloat16)
    low = (table - high.astype(np.float64)).astype(ml_dtypes.bfloat16)
    return np.stack([high, low])


def left_table(cosines, sines):
    high, low = two(np.concatenate([cosines, sines], 0))
    return np.concatenate([high, low, high], 1)


def right_table(table):
    high, low = two(table)
    return np.concatenate([high, high, low], 0)


def depth_order(depth):
    order = [0, depth // 2]
    for k in range(1, depth // 2):
        order += [k, depth - k]
    return np.array(order)


def phase_tables(rows, columns, length):
    angles = 2.0 * math.pi / length * (np.outer(rows, columns) % length)
    return np.cos(angles), np.sin(angles)


@functools.lru_cache(None)
def tables(depth, by, bx):
    half = bx // 2
    norm = 1.0 / math.sqrt(depth * by * bx)
    c, s = phase_tables(np.arange(bx), np.arange(half), bx)
    alternate = 1.0 - 2.0 * (np.arange(bx) % 2)
    imag = -s
    imag[:, 0] = alternate
    x_forward = np.concatenate([c, imag], 1)
    weights = np.where(np.arange(half) == 0, 1.0, 2.0)
    imag = -s * weights
    imag[:, 0] = alternate
    x_back = np.concatenate([c * weights, imag], 1).T * norm
    zc, zs = phase_tables(depth_order(depth), np.arange(depth), depth)
    eye = np.eye(SUB)
    yc, ys = phase_tables(np.arange(by), np.arange(by), by)
    return dict(
        x_forward=two(x_forward).reshape(2 * bx, bx),
        x_back=right_table(x_back),
        z_forward=left_table(np.kron(zc, eye), np.kron(zs, eye)),
        z_back=left_table(np.kron(zc.T, eye), np.kron(zs.T, eye)),
        y_forward=left_table(yc * norm, ys * norm),
        y_back=left_table(yc, ys),
    )


def dot(a, b):
    return jnp.dot(a, b, preferred_element_type=F32)


def split(a):
    high = a.astype(BF16)
    return high, (a - high.astype(F32)).astype(BF16)


def left_mix(table_ref, field):
    high, low = field
    both = dot(table_ref[...], jnp.concatenate([high, high, low], 0))
    size = table_ref.shape[0] // 2
    return both[:size], both[size:]


def right_mix(field, table_ref):
    high, low = field
    return dot(jnp.concatenate([high, low, high], 1), table_ref[...])


def inverse(a):
    guess = pl.reciprocal(a, approx=True)
    return guess * (2.0 - a * guess)


def params():
    return pltpu.CompilerParams(vmem_limit_bytes=LIMIT)


def cost(flops, bytes_accessed, transcendentals=0):
    return pl.CostEstimate(
        flops=int(flops) // EARLY,
        bytes_accessed=int(bytes_accessed) // EARLY,
        transcendentals=int(transcendentals) // EARLY,
    )


def whole(array):
    zeros = (0,) * array.ndim
    return pl.BlockSpec(array.shape, lambda *_: zeros)


def forward_kernel(obs_ref, x_ref, z_ref, *rest):
    out_refs, held = rest[:-1], rest[-1]
    _, depth, rows, width = obs_ref.shape
    half = width // 2
    group = out_refs[0].shape[0]
    lane = lax.broadcasted_iota(jnp.int32, (1, width), 1)
    centre = jnp.where(lane == 0, CENTRE * width, 0.0).astype(F32)
    flat = obs_ref[0].reshape(depth * rows, width)
    mixed = dot(jnp.concatenate([flat, flat], 1), x_ref[...]) - centre
    mixed = mixed.reshape(depth, rows, width)
    for at in range(0, rows, SUB):
        field = split(mixed[:, at : at + SUB, :].reshape(depth * SUB, width))
        cos_part, sin_part = left_mix(z_ref, field)
        real = cos_part[:, :half] + sin_part[:, half:]
        imag = cos_part[:, half:] - sin_part[:, :half]
        held[0, :, at : at + SUB, :] = real.reshape(depth, SUB, half)
        held[1, :, at : at + SUB, :] = imag.reshape(depth, SUB, half)
    for c in range(2):
        field = held[c].reshape(group, depth // group, rows, half)
        for p, out_ref in enumerate(out_refs):
            out_ref[:, 0, c] = field[:, 2 * p : 2 * p + 2]


def forward_spectra(observed, group, t):
    views, depth, rows, width = observed.shape
    chunks = depth // group // 2
    shape = (group, views, 2, 2, rows, width // 2)
    x_table, z_table = jnp.asarray(t["x_forward"]), jnp.asarray(t["z_forward"])
    return pl.pallas_call(
        forward_kernel,
        grid=(views,),
        out_shape=[jax.ShapeDtypeStruct(shape, F32)] * chunks,
        in_specs=[
            pl.BlockSpec((1,) + observed.shape[1:], lambda v: (v, 0, 0, 0)),
            whole(x_table),
            whole(z_table),
        ],
        out_specs=[pl.BlockSpec((group, 1) + shape[2:], lambda v: (0, v, 0, 0, 0, 0))] * chunks,
        scratch_shapes=[pltpu.VMEM((2, depth, rows, width // 2), F32)],
        compiler_params=params(),
        cost_estimate=cost(observed.size * 256 * 2 * 8, observed.size * 4),
        name="spectra_x_z",
    )(observed, x_table, z_table)


def cross_kernel(depth, first_ref, spec_ref, ref_ref, fwd_ref, back_ref, out_ref, held):
    group, _, _, _, rows, half = spec_ref.shape
    by = group * rows
    alone = first_ref[0] == 1
    lane0 = lax.broadcasted_iota(jnp.int32, (by, half), 1) == 0
    row0 = lax.broadcasted_iota(jnp.int32, (by, half), 0) == 0
    total = CENTRE * math.sqrt(depth * by * 2 * half)
    origin = jnp.logical_and(lane0, row0)

    def spectrum(ref):
        straight, turned = [], []
        for k in range(2):
            real = ref[:, 0, 0, k].astype(F32).reshape(by, half)
            imag = ref[:, 0, 1, k].astype(F32).reshape(by, half)
            field = split(jnp.concatenate([real, imag], 1))
            cos_part, sin_part = left_mix(fwd_ref, field)
            cos_real = cos_part[:, :half]
            if k == 0:
                cos_real = cos_real + jnp.where(jnp.logical_and(origin, alone), total, 0.0)
            straight.append((cos_real + sin_part[:, half:], cos_part[:, half:] - sin_part[:, :half]))
            turned.append((cos_real - sin_part[:, half:], cos_part[:, half:] + sin_part[:, :half]))
        out = []
        for k in range(2):
            real, imag = straight[k]
            other_real = jnp.where(alone, turned[k][0], turned[1 - k][0])
            other_imag = jnp.where(alone, turned[k][1], turned[1 - k][1])
            out.append(
                (
                    jnp.where(lane0, 0.5 * (real + other_real), real),
                    jnp.where(lane0, 0.5 * (imag - other_imag), imag),
                    0.5 * (imag + other_imag),
                    0.5 * (other_real - real),
                )
            )
        return out

    @pl.when(pl.program_id(0) == 0)
    def _():
        for k, member in enumerate(spectrum(ref_ref)):
            for i in range(4):
                held[k, i] = member[i]

    def cross(sr, si, rr, ri):
        magnitude = jnp.sqrt((sr * sr + si * si) * (rr * rr + ri * ri))
        scale = inverse(magnitude + 1.0)
        return (sr * rr + si * ri) * scale, (si * rr - sr * ri) * scale

    for k, member in enumerate(spectrum(spec_ref)):
        real, imag = cross(member[0], member[1], held[k, 0], held[k, 1])
        top_real, top_imag = cross(member[2], member[3], held[k, 2], held[k, 3])
        real = jnp.where(lane0, real - top_imag, real)
        imag = jnp.where(lane0, imag + top_real, imag)
        field = split(jnp.concatenate([real, imag], 1))
        cos_part, sin_part = left_mix(back_ref, field)
        real = cos_part[:, :half] - sin_part[:, half:]
        imag = cos_part[:, half:] + sin_part[:, :half]
        out_ref[:, 0, 0, k] = real.reshape(group, rows, half).astype(out_ref.dtype)
        out_ref[:, 0, 1, k] = imag.reshape(group, rows, half).astype(out_ref.dtype)


def cross_spectra(first, depth, turned, ref_turned, t):
    group, views, _, _, rows, half = turned.shape
    by = group * rows
    fwd, back = jnp.asarray(t["y_forward"]), jnp.asarray(t["y_back"])
    block = (group, 1, 2, 2, rows, half)
    return pl.pallas_call(
        functools.partial(cross_kernel, depth),
        grid=(views,),
        out_shape=jax.ShapeDtypeStruct(turned.shape, F32),
        in_specs=[
            pl.BlockSpec(memory_space=pltpu.SMEM),
            pl.BlockSpec(block, lambda v: (0, v, 0, 0, 0, 0)),
            pl.BlockSpec(block, lambda v: (0, 0, 0, 0, 0, 0)),
            whole(fwd),
            whole(back),
        ],
        out_specs=pl.BlockSpec(block, lambda v: (0, v, 0, 0, 0, 0)),
        scratch_shapes=[pltpu.VMEM((2, 4, by, half), F32)],
        compiler_params=params(),
        cost_estimate=cost(turned.size * 256 * 2 * 12, turned.size * 4, turned.size),
        name="cross_y",
    )(first, turned, ref_turned, fwd, back)


def inverse_kernel(*refs):
    back_refs, (z_ref, x_ref, out_ref, held) = refs[:-4], refs[-4:]
    group, _, _, _, rows, half = back_refs[0].shape
    depth = group * 2 * len(back_refs)
    for c in range(2):
        field = jnp.concatenate([ref[:, 0, c] for ref in back_refs], 1)
        held[c] = field.reshape(depth, rows, half)
    fields = []
    for at in range(0, rows, SUB):
        real = held[0, :, at : at + SUB, :].reshape(depth * SUB, half)
        imag = held[1, :, at : at + SUB, :].reshape(depth * SUB, half)
        field = split(jnp.concatenate([real, imag], 1))
        cos_part, sin_part = left_mix(z_ref, field)
        real = cos_part[:, :half] - sin_part[:, half:]
        imag = cos_part[:, half:] + sin_part[:, :half]
        fields.append(jnp.concatenate([real, imag], 1))
    result = right_mix(split(jnp.concatenate(fields, 0)), x_ref)
    size = depth * SUB
    for at in range(0, rows, SUB):
        part = result[at // SUB * size : (at // SUB + 1) * size]
        out_ref[0, :, at : at + SUB, :] = part.reshape(depth, SUB, 2 * half)


def inverse_spectra(backs, t):
    group, views, _, _, rows, half = backs[0].shape
    depth = group * 2 * len(backs)
    shape = (views, depth, rows, 2 * half)
    z_table, x_table = jnp.asarray(t["z_back"]), jnp.asarray(t["x_back"])
    return pl.pallas_call(
        inverse_kernel,
        grid=(views,),
        out_shape=jax.ShapeDtypeStruct(shape, F32),
        in_specs=[
            *[pl.BlockSpec((group, 1) + b.shape[2:], lambda v: (0, v, 0, 0, 0, 0)) for b in backs],
            whole(z_table),
            whole(x_table),
        ],
        out_specs=pl.BlockSpec((1,) + shape[1:], lambda v: (v, 0, 0, 0)),
        scratch_shapes=[pltpu.VMEM((2, depth, rows, half), F32)],
        compiler_params=params(),
        cost_estimate=cost(math.prod(shape) * 256 * 2 * 9, math.prod(shape) * 8),
        name="surface_z_x",
    )(*backs, z_table, x_table)


def by_tap(row, offsets):
    summed = jnp.zeros(offsets.shape, F32)
    for i in range(TAPS):
        summed = jnp.where(offsets == i, row(i), summed)
    return summed


def table_kernel(depth, group_ref, map_ref, shift_ref, taps_ref, zyf_ref, zyb_ref, xf_ref, xb_ref):
    width = xf_ref.shape[-1]
    size = depth * SUB
    view = map_ref[group_ref[0] * pl.num_programs(0) + pl.program_id(0)]
    shift_z, shift_x = shift_ref[view, 0], shift_ref[view, 1]

    def taps(axis):
        return lambda i: taps_ref[view, axis * TAPS + i]

    def places(rows, columns):
        shape = (rows, columns)
        return [lax.broadcasted_iota(jnp.int32, shape, d) for d in range(2)]

    row, col = places(depth, size)
    z_off = lax.shift_right_logical(col, 3) - row + 7
    z_pair = by_tap(taps(0), z_off - shift_z), by_tap(taps(0), 14 - z_off - shift_z)
    row, col = places(SUB, size)
    for j in range(3):
        y_off = SUB * (j - 1) + jnp.bitwise_and(col, SUB - 1) - row + 7
        y_pair = by_tap(taps(1), y_off), by_tap(taps(1), 14 - y_off)
        for ref, z, y in zip((zyf_ref, zyb_ref), z_pair, y_pair):
            both = (z[:, None, :] * y[None]).reshape(size, size)
            ref[0, j * size : (j + 1) * size] = both.astype(BF16)
    row, col = places(width, width)
    x_off = row - col + 7
    xf_ref[0] = by_tap(taps(2), x_off - shift_x).astype(BF16)
    xb_ref[0] = by_tap(taps(2), 14 - x_off - shift_x).astype(BF16)


def view_block(array):
    zeros = (0,) * (array.ndim - 1)
    return pl.BlockSpec((1,) + array.shape[1:], lambda v: (v,) + zeros)


def blur_tables(group_index, view_map, view_shifts, psf_taps, views, depth, width):
    size = depth * SUB
    zy = jax.ShapeDtypeStruct((views, 3 * size, size), BF16)
    x = jax.ShapeDtypeStruct((views, width, width), BF16)
    return pl.pallas_call(
        functools.partial(table_kernel, depth),
        grid=(views,),
        out_shape=[zy, zy, x, x],
        in_specs=[pl.BlockSpec(memory_space=pltpu.SMEM)] * 4,
        out_specs=[view_block(zy), view_block(zy), view_block(x), view_block(x)],
        compiler_params=params(),
        cost_estimate=cost(views * size * size * 100, views * size * size * 16),
        name="blur_tables",
    )(group_index.reshape(1), view_map, view_shifts, psf_taps.reshape(psf_taps.shape[0], -1))


def blur(pieces, zy_ref, x_ref, total, use):
    count = len(pieces) - 2
    size = zy_ref.shape[2]
    for b, piece in enumerate(pieces):
        steps = [j for j in range(3) if 0 <= b - j < count]
        table = zy_ref[0, steps[0] * size : (steps[-1] + 1) * size]
        table = jnp.concatenate([table] * len(piece), 1)
        mixed = dot(table, jnp.concatenate(piece, 0) if len(piece) > 1 else piece[0])
        for j in steps:
            part = mixed[(j - steps[0]) * size : (j - steps[0] + 1) * size]
            if j == 0:
                total[b - j] = part
            elif j == 1:
                total[b - j] += part
            else:
                done = dot(jnp.concatenate(split(total[b - j] + part), 0), x_ref[0])
                use(b - j, done[:size] + done[size:])


def join_kernel(
    est_ref, low_ref, high_ref, obs_ref, obs_low_ref, obs_high_ref,
    zyf_ref, zyb_ref, xf_ref, xb_ref, out_ref, held, total, ratio, parts,
):
    depth, rows, width = est_ref.shape
    size = depth * SUB
    count = rows // SUB
    held[...] = obs_ref[0].astype(F32)
    pieces = [(low_ref[0],), (low_ref[1],)]
    first = pl.program_id(0) == 0

    @pl.when(first)
    def _():
        for b in range(count):
            block = est_ref[:, b * SUB : (b + 1) * SUB, :].reshape(size, width)
            parts[b, 0], parts[b, 1] = split(block)

    pieces += [(parts[b, 0], parts[b, 1]) for b in range(count)]
    pieces += [(high_ref[0],), (high_ref[1],)]

    def keep_ratio(b, blurred):
        if b == 0:
            seen = obs_low_ref[0].astype(F32)
        elif b == count + 1:
            seen = obs_high_ref[0].astype(F32)
        else:
            seen = held[:, (b - 1) * SUB : b * SUB, :].reshape(size, width)
        value = seen * inverse(blurred)
        if b in (0, count + 1):
            value = jnp.where(seen > 0.0, value, 0.0)
        ratio[b] = value.astype(BF16)

    blur(pieces, zyf_ref, xf_ref, total, keep_ratio)

    def keep_update(b, update):
        spot = (slice(None), slice(b * SUB, (b + 1) * SUB), slice(None))
        update = update.reshape(depth, SUB, width)
        out_ref[spot] = jnp.where(first, update, update * out_ref[spot])

    pieces = [(ratio[b],) for b in range(count + 2)]
    blur(pieces, zyb_ref, xb_ref, total, keep_update)


def join_views(estimate, sides, observed, obs_sides, blurs):
    depth, rows, width = estimate.shape
    size = depth * SUB
    count = rows // SUB
    args = (estimate,) + tuple(sides) + (observed,) + tuple(obs_sides) + tuple(blurs)
    side = pl.BlockSpec((2, size, width), lambda v: (0, 0, 0))
    obs_side = pl.BlockSpec((1, size, width), lambda v: (v + 2, 0, 0))
    return pl.pallas_call(
        join_kernel,
        grid=(observed.shape[0],),
        out_shape=jax.ShapeDtypeStruct(estimate.shape, F32),
        in_specs=[whole(estimate), side, side, view_block(observed), obs_side, obs_side]
        + [view_block(a) for a in blurs],
        out_specs=whole(estimate),
        scratch_shapes=[
            pltpu.VMEM((depth, rows, width), F32),
            pltpu.VMEM((count + 2, size, width), F32),
            pltpu.VMEM((count + 2, size, width), BF16),
            pltpu.VMEM((count, 2, size, width), BF16),
        ],
        compiler_params=params(),
        cost_estimate=cost(observed.size * 256 * 2 * 20, observed.size * 8, observed.size),
        name="join_views",
    )(*args)


def blocks_of(rows_of, depth, count, width):
    shape = rows_of.shape[:-3]
    split_up = rows_of.astype(BF16).reshape(shape + (depth, count, SUB, width))
    return jnp.swapaxes(split_up, -4, -3).reshape(shape + (count, depth * SUB, width))


def from_sides(head, tail):
    count = lax.axis_size("gz")
    low = lax.ppermute(tail, "gz", [(i, i + 1) for i in range(count - 1)])
    high = lax.ppermute(head, "gz", [(i + 1, i) for i in range(count - 1)])
    return low, high


def from_partner(array):
    count = lax.axis_size("view")
    return lax.ppermute(array, "view", [(i, count - 1 - i) for i in range(count)])


def on_device(observed, initial, psf_taps, view_shifts, view_map):
    local_views = observed.shape[0]
    depth, rows, width = initial.shape
    gz = lax.axis_size("gz")
    t = tables(depth, rows * gz, width)
    group_index = lax.axis_index("view")
    all_slots = jnp.arange(view_map.shape[0], dtype=jnp.int32)
    ref_slot = jnp.sum(jnp.where(view_map == 0, all_slots, 0))
    ref_group = ref_slot // local_views
    ref_local = ref_slot % local_views

    def est_ends(estimate):
        head = blocks_of(estimate[:, : 2 * SUB], depth, 2, width)
        tail = blocks_of(estimate[:, rows - 2 * SUB :], depth, 2, width)
        return head, tail

    ends = (
        blocks_of(observed[:, :, :SUB], depth, 1, width)[:, 0],
        blocks_of(observed[:, :, rows - SUB :], depth, 1, width)[:, 0],
    )
    obs_sides = from_sides(*[jnp.concatenate(e, 0) for e in zip(est_ends(initial), ends)])
    blurs = blur_tables(group_index, view_map, view_shifts, psf_taps, local_views, depth, width)

    def product_of(estimate, sides):
        return join_views(estimate, sides, observed, obs_sides, blurs)

    def updated(estimate, product):
        product = product * from_partner(product)
        return estimate * jnp.exp(jnp.log(product) / VIEWS)

    def exchanged(array):
        array = array.astype(SENT)
        return lax.all_to_all(array, "gz", split_axis=0, concat_axis=0, tiled=True)

    def crossed(p, member):
        mine = lax.dynamic_index_in_dim(member, ref_local, 1, keepdims=True)
        ref_turned = jnp.where(group_index == ref_group, mine, from_partner(mine)).astype(F32)
        first = jnp.logical_and(lax.axis_index("gz") == 0, p == 0).astype(jnp.int32).reshape(1)
        return cross_spectra(first, depth, member.astype(F32), ref_turned, t).astype(SENT)

    after = lax.optimization_barrier
    turned = [exchanged(sent) for sent in forward_spectra(observed, gz, t)]
    turned[0], blurs = after((turned[0], blurs))
    mixed = [crossed(0, turned[0])]
    estimate, mixed[0] = after((initial, mixed[0]))
    estimate = updated(estimate, product_of(estimate, obs_sides))
    estimate, turned[1:] = after((estimate, turned[1:]))
    sides = from_sides(*est_ends(estimate))
    mixed += [crossed(p, turned[p]) for p in range(1, len(turned))]
    mixed[-1], sides, estimate = after((mixed[-1], sides, estimate))
    backs = [exchanged(member) for member in mixed]
    for step in range(1, ITERS):
        if step > 1:
            sides = from_sides(*est_ends(estimate))
        estimate = updated(estimate, product_of(estimate, sides))
    surfaces = inverse_spectra([b.astype(F32) for b in backs], t)
    return estimate, surfaces


def solution(mesh):
    placed = (P("view", "parts", "gz", None), P("parts", "gz", None), P(), P(), P())
    return jax.shard_map(
        on_device,
        mesh=mesh,
        in_specs=placed,
        out_specs=(P("parts", "gz", None), P("view", "parts", "gz", None)),
        check_vma=False,
    )
```

```python
import functools
import math

import jax
import jax.numpy as jnp
import ml_dtypes
import numpy as np
from jax import lax
from jax.experimental import pallas as pl
from jax.experimental.pallas import tpu as pltpu
from jax.sharding import PartitionSpec as P

VIEWS = 8
BX = 256
ITERS = 2
TAPS = 15
SUB = 8
CENTRE = 1.1
F32 = jnp.float32
BF16 = jnp.bfloat16
SENT = jnp.float16
LIMIT = 56 * 1024 * 1024


def two(table):
    high = table.astype(ml_dtypes.bfloat16)
    low = (table - high.astype(np.float64)).astype(ml_dtypes.bfloat16)
    return np.stack([high, low])


def left_table(cosines, sines):
    high, low = two(np.concatenate([cosines, sines], 0))
    return np.concatenate([high, low, high], 1)


def right_table(table):
    high, low = two(table)
    return np.concatenate([high, high, low], 0)


def depth_order(depth):
    order = [0, depth // 2]
    for k in range(1, depth // 2):
        order += [k, depth - k]
    return np.array(order)


def phase_tables(rows, columns, length):
    angles = 2.0 * math.pi / length * (np.outer(rows, columns) % length)
    return np.cos(angles), np.sin(angles)


@functools.lru_cache(None)
def tables(depth, by, bx):
    half = bx // 2
    norm = 1.0 / math.sqrt(depth * by * bx)
    c, s = phase_tables(np.arange(bx), np.arange(half), bx)
    alternate = 1.0 - 2.0 * (np.arange(bx) % 2)
    imag = -s
    imag[:, 0] = alternate
    x_forward = np.concatenate([c, imag], 1)
    weights = np.where(np.arange(half) == 0, 1.0, 2.0)
    imag = -s * weights
    imag[:, 0] = alternate
    x_back = np.concatenate([c * weights, imag], 1).T * norm
    zc, zs = phase_tables(depth_order(depth), np.arange(depth), depth)
    eye = np.eye(SUB)
    yc, ys = phase_tables(np.arange(by), np.arange(by), by)
    return dict(
        x_forward=two(x_forward).reshape(2 * bx, bx),
        x_back=right_table(x_back),
        z_forward=left_table(np.kron(zc, eye), np.kron(zs, eye)),
        z_back=left_table(np.kron(zc.T, eye), np.kron(zs.T, eye)),
        y_forward=left_table(yc * norm, ys * norm),
        y_back=left_table(yc, ys),
    )


def dot(a, b):
    return jnp.dot(a, b, preferred_element_type=F32)


def split(a):
    high = a.astype(BF16)
    return high, (a - high.astype(F32)).astype(BF16)


def left_mix(table_ref, field):
    high, low = field
    both = dot(table_ref[...], jnp.concatenate([high, high, low], 0))
    size = table_ref.shape[0] // 2
    return both[:size], both[size:]


def right_mix(field, table_ref):
    high, low = field
    return dot(jnp.concatenate([high, low, high], 1), table_ref[...])


def inverse(a):
    guess = pl.reciprocal(a, approx=True)
    return guess * (2.0 - a * guess)


def params():
    return pltpu.CompilerParams(vmem_limit_bytes=LIMIT)


def cost(flops, bytes_accessed, transcendentals=0):
    return pl.CostEstimate(
        flops=int(flops),
        bytes_accessed=int(bytes_accessed),
        transcendentals=int(transcendentals),
    )


def whole(array):
    zeros = (0,) * array.ndim
    return pl.BlockSpec(array.shape, lambda *_: zeros)


def forward_kernel(obs_ref, x_ref, z_ref, *rest):
    out_refs, held = rest[:-1], rest[-1]
    _, depth, rows, width = obs_ref.shape
    half = width // 2
    group = out_refs[0].shape[0]
    lane = lax.broadcasted_iota(jnp.int32, (1, width), 1)
    centre = jnp.where(lane == 0, CENTRE * width, 0.0).astype(F32)
    flat = obs_ref[0].reshape(depth * rows, width)
    mixed = dot(jnp.concatenate([flat, flat], 1), x_ref[...]) - centre
    mixed = mixed.reshape(depth, rows, width)
    for at in range(0, rows, SUB):
        field = split(mixed[:, at : at + SUB, :].reshape(depth * SUB, width))
        cos_part, sin_part = left_mix(z_ref, field)
        real = cos_part[:, :half] + sin_part[:, half:]
        imag = cos_part[:, half:] - sin_part[:, :half]
        held[0, :, at : at + SUB, :] = real.reshape(depth, SUB, half)
        held[1, :, at : at + SUB, :] = imag.reshape(depth, SUB, half)
    for c in range(2):
        field = held[c].reshape(group, depth // group, rows, half)
        for p, out_ref in enumerate(out_refs):
            out_ref[:, 0, c] = field[:, 2 * p : 2 * p + 2]


def forward_spectra(observed, group, t):
    views, depth, rows, width = observed.shape
    chunks = depth // group // 2
    shape = (group, views, 2, 2, rows, width // 2)
    x_table, z_table = jnp.asarray(t["x_forward"]), jnp.asarray(t["z_forward"])
    return pl.pallas_call(
        forward_kernel,
        grid=(views,),
        out_shape=[jax.ShapeDtypeStruct(shape, F32)] * chunks,
        in_specs=[
            pl.BlockSpec((1,) + observed.shape[1:], lambda v: (v, 0, 0, 0)),
            whole(x_table),
            whole(z_table),
        ],
        out_specs=[pl.BlockSpec((group, 1) + shape[2:], lambda v: (0, v, 0, 0, 0, 0))] * chunks,
        scratch_shapes=[pltpu.VMEM((2, depth, rows, width // 2), F32)],
        compiler_params=params(),
        cost_estimate=cost(observed.size * 256 * 2 * 8, observed.size * 4),
        name="spectra_x_z",
    )(observed, x_table, z_table)


def cross_kernel(depth, first_ref, spec_ref, ref_ref, fwd_ref, back_ref, out_ref, held):
    group, _, _, _, rows, half = spec_ref.shape
    by = group * rows
    alone = first_ref[0] == 1
    lane0 = lax.broadcasted_iota(jnp.int32, (by, half), 1) == 0
    row0 = lax.broadcasted_iota(jnp.int32, (by, half), 0) == 0
    total = CENTRE * math.sqrt(depth * by * 2 * half)
    origin = jnp.logical_and(lane0, row0)

    def spectrum(ref):
        straight, turned = [], []
        for k in range(2):
            real = ref[:, 0, 0, k].astype(F32).reshape(by, half)
            imag = ref[:, 0, 1, k].astype(F32).reshape(by, half)
            field = split(jnp.concatenate([real, imag], 1))
            cos_part, sin_part = left_mix(fwd_ref, field)
            cos_real = cos_part[:, :half]
            if k == 0:
                cos_real = cos_real + jnp.where(jnp.logical_and(origin, alone), total, 0.0)
            straight.append((cos_real + sin_part[:, half:], cos_part[:, half:] - sin_part[:, :half]))
            turned.append((cos_real - sin_part[:, half:], cos_part[:, half:] + sin_part[:, :half]))
        out = []
        for k in range(2):
            real, imag = straight[k]
            other_real = jnp.where(alone, turned[k][0], turned[1 - k][0])
            other_imag = jnp.where(alone, turned[k][1], turned[1 - k][1])
            out.append(
                (
                    jnp.where(lane0, 0.5 * (real + other_real), real),
                    jnp.where(lane0, 0.5 * (imag - other_imag), imag),
                    0.5 * (imag + other_imag),
                    0.5 * (other_real - real),
                )
            )
        return out

    @pl.when(pl.program_id(0) == 0)
    def _():
        for k, member in enumerate(spectrum(ref_ref)):
            for i in range(4):
                held[k, i] = member[i]

    def cross(sr, si, rr, ri):
        magnitude = jnp.sqrt((sr * sr + si * si) * (rr * rr + ri * ri))
        scale = inverse(magnitude + 1.0)
        return (sr * rr + si * ri) * scale, (si * rr - sr * ri) * scale

    for k, member in enumerate(spectrum(spec_ref)):
        real, imag = cross(member[0], member[1], held[k, 0], held[k, 1])
        top_real, top_imag = cross(member[2], member[3], held[k, 2], held[k, 3])
        real = jnp.where(lane0, real - top_imag, real)
        imag = jnp.where(lane0, imag + top_real, imag)
        field = split(jnp.concatenate([real, imag], 1))
        cos_part, sin_part = left_mix(back_ref, field)
        real = cos_part[:, :half] - sin_part[:, half:]
        imag = cos_part[:, half:] + sin_part[:, :half]
        out_ref[:, 0, 0, k] = real.reshape(group, rows, half).astype(out_ref.dtype)
        out_ref[:, 0, 1, k] = imag.reshape(group, rows, half).astype(out_ref.dtype)


def cross_spectra(first, depth, turned, ref_turned, t):
    group, views, _, _, rows, half = turned.shape
    by = group * rows
    fwd, back = jnp.asarray(t["y_forward"]), jnp.asarray(t["y_back"])
    block = (group, 1, 2, 2, rows, half)
    return pl.pallas_call(
        functools.partial(cross_kernel, depth),
        grid=(views,),
        out_shape=jax.ShapeDtypeStruct(turned.shape, F32),
        in_specs=[
            pl.BlockSpec(memory_space=pltpu.SMEM),
            pl.BlockSpec(block, lambda v: (0, v, 0, 0, 0, 0)),
            pl.BlockSpec(block, lambda v: (0, 0, 0, 0, 0, 0)),
            whole(fwd),
            whole(back),
        ],
        out_specs=pl.BlockSpec(block, lambda v: (0, v, 0, 0, 0, 0)),
        scratch_shapes=[pltpu.VMEM((2, 4, by, half), F32)],
        compiler_params=params(),
        cost_estimate=cost(turned.size * 256 * 2 * 12, turned.size * 4, turned.size),
        name="cross_y",
    )(first, turned, ref_turned, fwd, back)


def inverse_kernel(*refs):
    back_refs, (z_ref, x_ref, out_ref, held) = refs[:-4], refs[-4:]
    group, _, _, _, rows, half = back_refs[0].shape
    depth = group * 2 * len(back_refs)
    for c in range(2):
        field = jnp.concatenate([ref[:, 0, c] for ref in back_refs], 1)
        held[c] = field.reshape(depth, rows, half)
    fields = []
    for at in range(0, rows, SUB):
        real = held[0, :, at : at + SUB, :].reshape(depth * SUB, half)
        imag = held[1, :, at : at + SUB, :].reshape(depth * SUB, half)
        field = split(jnp.concatenate([real, imag], 1))
        cos_part, sin_part = left_mix(z_ref, field)
        real = cos_part[:, :half] - sin_part[:, half:]
        imag = cos_part[:, half:] + sin_part[:, :half]
        fields.append(jnp.concatenate([real, imag], 1))
    result = right_mix(split(jnp.concatenate(fields, 0)), x_ref)
    size = depth * SUB
    for at in range(0, rows, SUB):
        part = result[at // SUB * size : (at // SUB + 1) * size]
        out_ref[0, :, at : at + SUB, :] = part.reshape(depth, SUB, 2 * half)


def inverse_spectra(backs, t):
    group, views, _, _, rows, half = backs[0].shape
    depth = group * 2 * len(backs)
    shape = (views, depth, rows, 2 * half)
    z_table, x_table = jnp.asarray(t["z_back"]), jnp.asarray(t["x_back"])
    return pl.pallas_call(
        inverse_kernel,
        grid=(views,),
        out_shape=jax.ShapeDtypeStruct(shape, F32),
        in_specs=[
            *[pl.BlockSpec((group, 1) + b.shape[2:], lambda v: (0, v, 0, 0, 0, 0)) for b in backs],
            whole(z_table),
            whole(x_table),
        ],
        out_specs=pl.BlockSpec((1,) + shape[1:], lambda v: (v, 0, 0, 0)),
        scratch_shapes=[pltpu.VMEM((2, depth, rows, half), F32)],
        compiler_params=params(),
        cost_estimate=cost(math.prod(shape) * 256 * 2 * 9, math.prod(shape) * 8),
        name="surface_z_x",
    )(*backs, z_table, x_table)


def by_tap(row, offsets):
    summed = jnp.zeros(offsets.shape, F32)
    for i in range(TAPS):
        summed = jnp.where(offsets == i, row(i), summed)
    return summed


def table_kernel(depth, group_ref, map_ref, shift_ref, taps_ref, zyf_ref, zyb_ref, xf_ref, xb_ref):
    width = xf_ref.shape[-1]
    size = depth * SUB
    view = map_ref[group_ref[0] * pl.num_programs(0) + pl.program_id(0)]
    shift_z, shift_x = shift_ref[view, 0], shift_ref[view, 1]

    def taps(axis):
        return lambda i: taps_ref[view, axis * TAPS + i]

    def places(rows, columns):
        shape = (rows, columns)
        return [lax.broadcasted_iota(jnp.int32, shape, d) for d in range(2)]

    row, col = places(depth, size)
    z_off = lax.shift_right_logical(col, 3) - row + 7
    z_pair = by_tap(taps(0), z_off - shift_z), by_tap(taps(0), 14 - z_off - shift_z)
    row, col = places(SUB, size)
    for j in range(3):
        y_off = SUB * (j - 1) + jnp.bitwise_and(col, SUB - 1) - row + 7
        y_pair = by_tap(taps(1), y_off), by_tap(taps(1), 14 - y_off)
        for ref, z, y in zip((zyf_ref, zyb_ref), z_pair, y_pair):
            both = (z[:, None, :] * y[None]).reshape(size, size)
            ref[0, j * size : (j + 1) * size] = both.astype(BF16)
    row, col = places(width, width)
    x_off = row - col + 7
    xf_ref[0] = by_tap(taps(2), x_off - shift_x).astype(BF16)
    xb_ref[0] = by_tap(taps(2), 14 - x_off - shift_x).astype(BF16)


def view_block(array):
    zeros = (0,) * (array.ndim - 1)
    return pl.BlockSpec((1,) + array.shape[1:], lambda v: (v,) + zeros)


def blur_tables(group_index, view_map, view_shifts, psf_taps, views, depth, width):
    size = depth * SUB
    zy = jax.ShapeDtypeStruct((views, 3 * size, size), BF16)
    x = jax.ShapeDtypeStruct((views, width, width), BF16)
    return pl.pallas_call(
        functools.partial(table_kernel, depth),
        grid=(views,),
        out_shape=[zy, zy, x, x],
        in_specs=[pl.BlockSpec(memory_space=pltpu.SMEM)] * 4,
        out_specs=[view_block(zy), view_block(zy), view_block(x), view_block(x)],
        compiler_params=params(),
        cost_estimate=cost(views * size * size * 100, views * size * size * 16),
        name="blur_tables",
    )(group_index.reshape(1), view_map, view_shifts, psf_taps.reshape(psf_taps.shape[0], -1))


def blur(pieces, zy_ref, x_ref, total, use):
    count = len(pieces) - 2
    size = zy_ref.shape[2]
    for b, piece in enumerate(pieces):
        steps = [j for j in range(3) if 0 <= b - j < count]
        table = zy_ref[0, steps[0] * size : (steps[-1] + 1) * size]
        table = jnp.concatenate([table] * len(piece), 1)
        mixed = dot(table, jnp.concatenate(piece, 0) if len(piece) > 1 else piece[0])
        for j in steps:
            part = mixed[(j - steps[0]) * size : (j - steps[0] + 1) * size]
            if j == 0:
                total[b - j] = part
            elif j == 1:
                total[b - j] += part
            else:
                done = dot(jnp.concatenate(split(total[b - j] + part), 0), x_ref[0])
                use(b - j, done[:size] + done[size:])


def join_kernel(
    est_ref, low_ref, high_ref, obs_ref, obs_low_ref, obs_high_ref,
    zyf_ref, zyb_ref, xf_ref, xb_ref, out_ref, held, total, ratio, parts,
):
    depth, rows, width = est_ref.shape
    size = depth * SUB
    count = rows // SUB
    held[...] = obs_ref[0].astype(F32)
    pieces = [(low_ref[0],), (low_ref[1],)]
    first = pl.program_id(0) == 0

    @pl.when(first)
    def _():
        for b in range(count):
            block = est_ref[:, b * SUB : (b + 1) * SUB, :].reshape(size, width)
            parts[b, 0], parts[b, 1] = split(block)

    pieces += [(parts[b, 0], parts[b, 1]) for b in range(count)]
    pieces += [(high_ref[0],), (high_ref[1],)]

    def keep_ratio(b, blurred):
        if b == 0:
            seen = obs_low_ref[0].astype(F32)
        elif b == count + 1:
            seen = obs_high_ref[0].astype(F32)
        else:
            seen = held[:, (b - 1) * SUB : b * SUB, :].reshape(size, width)
        value = seen * inverse(blurred)
        if b in (0, count + 1):
            value = jnp.where(seen > 0.0, value, 0.0)
        ratio[b] = value.astype(BF16)

    blur(pieces, zyf_ref, xf_ref, total, keep_ratio)

    def keep_update(b, update):
        spot = (slice(None), slice(b * SUB, (b + 1) * SUB), slice(None))
        update = update.reshape(depth, SUB, width)
        out_ref[spot] = jnp.where(first, update, update * out_ref[spot])

    pieces = [(ratio[b],) for b in range(count + 2)]
    blur(pieces, zyb_ref, xb_ref, total, keep_update)


def join_views(estimate, sides, observed, obs_sides, blurs):
    depth, rows, width = estimate.shape
    size = depth * SUB
    count = rows // SUB
    args = (estimate,) + tuple(sides) + (observed,) + tuple(obs_sides) + tuple(blurs)
    side = pl.BlockSpec((2, size, width), lambda v: (0, 0, 0))
    obs_side = pl.BlockSpec((1, size, width), lambda v: (v + 2, 0, 0))
    return pl.pallas_call(
        join_kernel,
        grid=(observed.shape[0],),
        out_shape=jax.ShapeDtypeStruct(estimate.shape, F32),
        in_specs=[whole(estimate), side, side, view_block(observed), obs_side, obs_side]
        + [view_block(a) for a in blurs],
        out_specs=whole(estimate),
        scratch_shapes=[
            pltpu.VMEM((depth, rows, width), F32),
            pltpu.VMEM((count + 2, size, width), F32),
            pltpu.VMEM((count + 2, size, width), BF16),
            pltpu.VMEM((count, 2, size, width), BF16),
        ],
        compiler_params=params(),
        cost_estimate=cost(observed.size * 256 * 2 * 20, observed.size * 8, observed.size),
        name="join_views",
    )(*args)


def blocks_of(rows_of, depth, count, width):
    shape = rows_of.shape[:-3]
    split_up = rows_of.astype(BF16).reshape(shape + (depth, count, SUB, width))
    return jnp.swapaxes(split_up, -4, -3).reshape(shape + (count, depth * SUB, width))


def from_sides(head, tail):
    count = lax.axis_size("gz")
    low = lax.ppermute(tail, "gz", [(i, i + 1) for i in range(count - 1)])
    high = lax.ppermute(head, "gz", [(i + 1, i) for i in range(count - 1)])
    return low, high


def from_partner(array):
    count = lax.axis_size("view")
    return lax.ppermute(array, "view", [(i, count - 1 - i) for i in range(count)])


def on_device(observed, initial, psf_taps, view_shifts, view_map):
    local_views = observed.shape[0]
    depth, rows, width = initial.shape
    gz = lax.axis_size("gz")
    t = tables(depth, rows * gz, width)
    group_index = lax.axis_index("view")
    all_slots = jnp.arange(view_map.shape[0], dtype=jnp.int32)
    ref_slot = jnp.sum(jnp.where(view_map == 0, all_slots, 0))
    ref_group = ref_slot // local_views
    ref_local = ref_slot % local_views

    def est_ends(estimate):
        head = blocks_of(estimate[:, : 2 * SUB], depth, 2, width)
        tail = blocks_of(estimate[:, rows - 2 * SUB :], depth, 2, width)
        return head, tail

    ends = (
        blocks_of(observed[:, :, :SUB], depth, 1, width)[:, 0],
        blocks_of(observed[:, :, rows - SUB :], depth, 1, width)[:, 0],
    )
    obs_sides = from_sides(*[jnp.concatenate(e, 0) for e in zip(est_ends(initial), ends)])
    blurs = blur_tables(group_index, view_map, view_shifts, psf_taps, local_views, depth, width)

    def joined(estimate, sides):
        product = join_views(estimate, sides, observed, obs_sides, blurs)
        product = product * from_partner(product)
        return estimate * jnp.exp(jnp.log(product) / VIEWS)

    def exchanged(array):
        return lax.all_to_all(array.astype(SENT), "gz", split_axis=0, concat_axis=0, tiled=True)

    estimate = joined(initial, obs_sides)
    turned = [exchanged(sent) for sent in forward_spectra(observed, gz, t)]
    backs = []
    for p, member in enumerate(turned):
        mine = lax.dynamic_index_in_dim(member, ref_local, 1, keepdims=True)
        ref_turned = jnp.where(group_index == ref_group, mine, from_partner(mine)).astype(F32)
        first = jnp.logical_and(lax.axis_index("gz") == 0, p == 0).astype(jnp.int32).reshape(1)
        crossed = cross_spectra(first, depth, member.astype(F32), ref_turned, t)
        backs.append(exchanged(crossed).astype(F32))
    for _ in range(1, ITERS):
        estimate = joined(estimate, from_sides(*est_ends(estimate)))
    surfaces = inverse_spectra(backs, t)
    return estimate, surfaces


def solution(mesh):
    placed = (P("view", "parts", "gz", None), P("parts", "gz", None), P(), P(), P())
    return jax.shard_map(
        on_device,
        mesh=mesh,
        in_specs=placed,
        out_specs=(P("parts", "gz", None), P("view", "parts", "gz", None)),
        check_vma=False,
    )
```
